512 devices in a mesh: node: 64 (over z, x, core), feat: 8 (over y).
Axes of the slice: x: 4, y: 8, z: 8, core: 2. Of those that a mesh axis runs over, the one named last changes fastest.
Arguments:
- features: bfloat16 [262144, 512], P('node', 'feat'), may hold values from -6 to 6
- weight: bfloat16 [512, 512], P('feat'), may hold values from -0.25 to 0.25
- tile_row: int32 [5120], P('node'), may hold values from 0 to 31
- tile_col: int32 [5120], P('node'), may hold values from 0 to 95
- tile_count: int32 [64], P('node'), may hold values from 40 to 80, as said below
- send_blocks: int32 [64, 64, 1], P('node'), may hold values from 0 to 31
- tile_values: bfloat16 [5120, 128, 128], P('node'), may hold values from -0.3125 to 0.3125
- upstream: bfloat16 [262144, 512], P('node', 'feat'), may hold values from -6 to 6
Outputs:
- features_grad: bfloat16 [262144, 512], P('node', 'feat')
- weight_grad: float32 [512, 512], P('feat')
The draws below stay inside these ranges and needn't reach their ends.
Inputs may be any that keep to these rules, and one draw needn't show every extreme that they name: `tile_count`: every partition has 40 or more live tiles, and one partition has exactly 80. Sixteen of the live tiles of each partition q are tiles that read the received slots of the 16 partitions (q + d) mod 64 for d in ±1, ±2, …, ±7, +8 and +32, one tile each; every other tile reads one of the partition's own blocks.
All inputs are finite; a program needn't handle non-finite values.
Results may differ from the reference program's by a relative error of at most 0.0061.
Values may be sent and summed in bfloat16 or wider, within the bound.
A program may use at most 64 MiB of HBM per device.

```python
import jax
import jax.numpy as jnp
from jax import lax

BLOCKS = 32
BLK = 128
FEAT = 512
SLOTS = 1
TILES = 80
NODES = 262144
N_NODE = 64


def live_counts(key):
    key_count = jax.random.fold_in(key, 5)
    first, second = jax.random.split(key_count)
    counts = jax.random.randint(first, (N_NODE,), TILES // 2, TILES + 1)
    full_at = jax.random.randint(second, (), 0, N_NODE)
    return counts.at[full_at].set(TILES).astype(jnp.int32)


def draw_tile_count(key, part):
    return live_counts(key)


def draw_tile_col(key, part):
    counts = live_counts(key)
    key = jax.random.fold_in(key, 7)
    key_slot, key_rand, key_order = jax.random.split(key, 3)
    reach = N_NODE // 4
    part_ids = jnp.arange(N_NODE, dtype=jnp.int32)[:, None]
    positions = jnp.arange(TILES, dtype=jnp.int32)[None, :]
    step_size = positions // 2 + 1
    offsets = jnp.where(positions % 2 == 0, step_size, N_NODE - step_size)
    offsets = jnp.where(positions == reach - 1, N_NODE // 2, offsets)
    peers = (part_ids + offsets) % N_NODE
    slot_pick = jax.random.randint(key_slot, (N_NODE, TILES), 0, SLOTS)
    cover = BLOCKS + peers * SLOTS + slot_pick
    local_cols = jax.random.randint(key_rand, (N_NODE, TILES), 0, BLOCKS)
    columns = jnp.where(positions < reach, cover, local_cols)
    scores = jax.random.randint(key_order, (N_NODE, TILES), 0, TILES) * TILES + positions
    scores = jnp.where(positions < counts[:, None], scores, scores + TILES * TILES)
    order = jnp.argsort(scores, axis=1, stable=True)
    columns = jnp.take_along_axis(columns, order, axis=1)
    return columns.reshape(-1).astype(jnp.int32)


def touch_ends(array, rng, low, largest):
    longest = array.shape.index(max(array.shape))
    spots = []
    for shift in (0, 1):
        where = [jax.random.randint(jax.random.fold_in(rng, axis), (), 0, length) for axis, length in enumerate(array.shape)]
        where[longest] = (where[longest] + shift) % array.shape[longest]
        spots.append(tuple(where))
    return array.at[spots[0]].set(low).at[spots[1]].set(largest)


def shard_levels(key, extent, cuts, low, top_value):
    def one(axis_at, shards_of):
        steps = jax.random.uniform(jax.random.fold_in(jax.random.fold_in(key, 6), axis_at), (shards_of,), jnp.float32, low / len(cuts), top_value / len(cuts))
        return jnp.repeat(jnp.exp(steps), extent[axis_at] // shards_of).reshape((-1,) + (1,) * (len(extent) - axis_at - 1))

    loudness = one(*cuts[0])
    for cut in cuts[1:]:
        loudness = loudness * one(*cut)
    return loudness


def centred(rng, shape, deviation, limit, cuts=(), kind=jnp.bfloat16):
    drawn = deviation * jax.random.normal(rng, shape, jnp.float32)
    if cuts:
        drawn = drawn * shard_levels(rng, shape, cuts, -0.22, 0.18)
    return jnp.clip(drawn, -limit, limit).astype(kind)


def setup_inputs(seed: int = 0) -> dict:
    arg_keys = jax.random.split(jax.random.key(seed), 9)
    return {
        "features": centred(arg_keys[0], (NODES, FEAT), 1.0, 6.0, ((0, 64), (1, 8))),
        "weight": centred(arg_keys[1], (FEAT, FEAT), FEAT ** -0.5, 0.25, ((0, 8),)),
        "tile_row": touch_ends(jax.random.randint(arg_keys[2], (N_NODE * TILES,), 0, BLOCKS), jax.random.fold_in(arg_keys[2], 1), 0, BLOCKS - 1).astype(jnp.int32),
        "tile_col": draw_tile_col(jax.random.fold_in(arg_keys[8], 71), 0),
        "tile_count": draw_tile_count(jax.random.fold_in(arg_keys[8], 71), 0),
        "send_blocks": touch_ends(jax.random.randint(arg_keys[5], (N_NODE, N_NODE, SLOTS), 0, BLOCKS), jax.random.fold_in(arg_keys[5], 1), 0, BLOCKS - 1).astype(jnp.int32),
        "tile_values": centred(arg_keys[6], (N_NODE * TILES, BLK, BLK), (3 * BLK) ** -0.5, 0.3125, ((0, 64),)),
        "upstream": centred(arg_keys[7], (NODES, FEAT), 1.0, 6.0, ((0, 64), (1, 8))),
    }


def reference(features, weight, tile_row, tile_col, tile_count, send_blocks, tile_values, upstream):
    blocked = features.reshape(N_NODE, BLOCKS, BLK, FEAT)
    row_ids = tile_row.reshape(N_NODE, TILES)
    col_ids = tile_col.reshape(N_NODE, TILES)
    tile_vals = tile_values.reshape(N_NODE, TILES, BLK, BLK)
    owners = jnp.arange(N_NODE).astype(jnp.int32)

    def agg_one(part_id):
        halo = blocked[owners[:, None], send_blocks[:, part_id, :]]
        table = jnp.concatenate([blocked[part_id], halo.reshape(N_NODE * SLOTS, BLK, FEAT)], 0)
        alive = (jnp.arange(TILES) < tile_count[part_id]).astype(jnp.float32)
        sources = table[col_ids[part_id]].astype(jnp.float32)
        terms = jnp.einsum('tij,tjf->tif', tile_vals[part_id].astype(jnp.float32), sources)
        terms = terms * alive[:, None, None]
        return jax.ops.segment_sum(terms, row_ids[part_id], num_segments=BLOCKS)
    aggregated = lax.map(agg_one, owners).reshape(N_NODE * BLOCKS * BLK, FEAT).astype(jnp.bfloat16)
    pre_act = jnp.dot(aggregated, weight, preferred_element_type=jnp.float32)
    sig = jax.nn.sigmoid(pre_act)
    grad_pre = (upstream.astype(jnp.float32) * sig * (1.0 + pre_act * (1.0 - sig))).astype(jnp.bfloat16)
    weight_grad = jnp.dot(aggregated.T, grad_pre, preferred_element_type=jnp.float32)
    weight_grad = weight_grad / jnp.sqrt(jnp.float32(N_NODE * BLOCKS * BLK))
    grad_agg = jnp.dot(grad_pre, weight.T, preferred_element_type=jnp.float32).astype(jnp.bfloat16)
    grad_blocks = grad_agg.reshape(N_NODE, BLOCKS, BLK, FEAT)
    slot_owner = jnp.repeat(owners, SLOTS)

    def back_one(totals, part_id):
        alive = (jnp.arange(TILES) < tile_count[part_id]).astype(jnp.float32)
        sources = grad_blocks[part_id][row_ids[part_id]].astype(jnp.float32)
        terms = jnp.einsum('tji,tjf->tif', tile_vals[part_id].astype(jnp.float32), sources)
        terms = terms * alive[:, None, None]
        scattered = jnp.zeros((BLOCKS + N_NODE * SLOTS, BLK, FEAT), jnp.float32).at[col_ids[part_id]].add(terms)
        totals = totals.at[part_id].add(scattered[:BLOCKS])
        targets = send_blocks[:, part_id, :].reshape(-1)
        totals = totals.at[slot_owner, targets].add(scattered[BLOCKS:])
        return (totals, None)
    start_totals = jnp.zeros((N_NODE, BLOCKS, BLK, FEAT), jnp.float32)
    totals, _ = lax.scan(back_one, start_totals, owners)
    features_grad = totals.reshape(N_NODE * BLOCKS * BLK, FEAT).astype(jnp.bfloat16)
    return (features_grad, weight_grad)
```

```python
import functools
import math

import jax
import jax.numpy as jnp
from jax import lax
from jax.experimental import pallas as pl
from jax.experimental.pallas import tpu as pltpu
from jax.sharding import PartitionSpec as P

MESH = pl.DeviceIdType.MESH
F32 = jnp.float32
BF16 = jnp.bfloat16
BLK = 128
CORES = 2
X_CHIPS = 4


def halo_offsets(node_count):
    near = [step for d in range(1, 8) for step in (d, -d)]
    return near + [8, 32]


class Plan:
    def __init__(self, blocks, width, tiles, feats, nodes, offsets, x_chips):
        self.blocks, self.width, self.tiles = blocks, width, tiles
        self.feats, self.nodes, self.offsets = feats, nodes, offsets
        self.halo = len(offsets)
        self.local = tiles - self.halo
        self.full = width * feats
        self.stages = blocks // (2 * feats)
        self.xs = x_chips
        self.zs = nodes // (CORES * x_chips)
        at = 0
        for name, size in (
            ("fl_t", self.local), ("fl_c", self.local), ("fl_k", self.local), ("fl_end", blocks),
            ("fh_t", self.halo), ("fh_s", self.halo), ("fh_k", self.halo), ("fh_end", blocks),
            ("bh_t", self.halo), ("bh_r", self.halo),
            ("bl_t", self.local), ("bl_r", self.local), ("bl_k", self.local), ("bl_end", blocks),
            ("r_s", self.halo), ("r_k", self.halo), ("r_end", blocks),
            ("send", self.halo),
        ):
            setattr(self, name, at)
            at += size
        self.length = at


def ordered(key, payloads, keep):
    rank = jnp.sum((key[None, :] < key[:, None]).astype(jnp.int32), axis=1)
    place = rank[None, :] == jnp.arange(keep, dtype=jnp.int32)[:, None]
    return [jnp.sum(jnp.where(place, p[None, :], 0), axis=1) for p in payloads]


def group_marks(group, count):
    follows = jnp.concatenate([jnp.zeros((1,), jnp.int32), (group[1:] == group[:-1]).astype(jnp.int32)])
    ids = jnp.arange(count, dtype=jnp.int32)[:, None]
    upto = jnp.sum((group[None, :] <= ids).astype(jnp.int32), axis=1)
    some = jnp.any(group[None, :] == ids, axis=1)
    return follows, jnp.where(some, upto, 0)


def index_lists(plan, tile_row, tile_col, tile_count, send_blocks):
    n = plan.nodes
    me = lax.axis_index("node")
    offsets = jnp.array(plan.offsets, jnp.int32)
    t = jnp.arange(plan.tiles, dtype=jnp.int32)
    alive = t < tile_count[0]
    local = alive & (tile_col < plan.blocks)
    read_from = plan.blocks + (me + offsets + n) % n
    is_halo = alive[None, :] & (tile_col[None, :] == read_from[:, None])
    bh_t = jnp.sum(jnp.where(is_halo, t[None, :], 0), axis=1)
    bh_r = jnp.sum(jnp.where(is_halo, tile_row[None, :], 0), axis=1)
    send_to = (me - offsets + n) % n
    sends = send_blocks[0, :, 0]
    nodes = jnp.arange(n, dtype=jnp.int32)
    send = jnp.sum(jnp.where(nodes[None, :] == send_to[:, None], sends[None, :], 0), axis=1)
    slot = jnp.arange(plan.halo, dtype=jnp.int32)

    row_or_none = jnp.where(local, tile_row, plan.blocks)
    col_or_none = jnp.where(local, tile_col, plan.blocks)
    fl_t, fl_r, fl_c = ordered(row_or_none * plan.tiles + t, (t, row_or_none, col_or_none), plan.local)
    fl_k, fl_end = group_marks(fl_r, plan.blocks)
    fh_t, fh_r, fh_s = ordered(bh_r * plan.halo + slot, (bh_t, bh_r, slot), plan.halo)
    fh_k, fh_end = group_marks(fh_r, plan.blocks)
    bl_t, bl_c, bl_r = ordered(col_or_none * plan.tiles + t, (t, col_or_none, row_or_none), plan.local)
    bl_k, bl_end = group_marks(bl_c, plan.blocks)
    r_s, r_c = ordered(send * plan.halo + slot, (slot, send), plan.halo)
    r_k, r_end = group_marks(r_c, plan.blocks)
    return jnp.concatenate(
        [fl_t, fl_c, fl_k, fl_end, fh_t, fh_s, fh_k, fh_end, bh_t, bh_r, bl_t, bl_r, bl_k, bl_end, r_s, r_k, r_end, send]
    )


def kernel(plan, idx, feats_hbm, up_hbm, w_hbm, tiles_hbm, out_ref, wout_ref, s):
    nf, nn, width = plan.feats, plan.nodes, plan.width
    zs, xs = plan.zs, plan.xs
    half = BLK // 2
    node, f = lax.axis_index("node"), lax.axis_index("feat")
    c = lax.rem(node, CORES)
    x = lax.rem(node // CORES, xs)
    z = node // (CORES * xs)

    def node_of(z_at, x_at, c_at):
        return (z_at * xs + x_at) * CORES + c_at

    def remote(src, dst, send_sem, recv_sem, to):
        return pltpu.make_async_remote_copy(
            src_ref=src, dst_ref=dst, send_sem=send_sem, recv_sem=recv_sem, device_id=to, device_id_type=MESH
        )

    get_feats = pltpu.make_async_copy(feats_hbm, s.table.at[pl.ds(0, plan.blocks)], s.get.at[0])
    get_up = pltpu.make_async_copy(up_hbm, s.up, s.get.at[1])
    get_w = pltpu.make_async_copy(w_hbm.at[pl.ds(c * (width // 2), width // 2)], s.wh.at[c, f], s.get.at[2])
    get_tiles = pltpu.make_async_copy(tiles_hbm, s.tiles, s.get.at[3])
    get_feats.start()
    get_up.start()
    get_w.start()
    get_tiles.start()

    near = sorted({d % nn for d in plan.offsets} | {-d % nn for d in plan.offsets})
    partners = [(lax.rem(node + d, nn), f) for d in near]
    partners += [(node, lax.rem(f + d, nf)) for d in range(1, nf)]
    partners += [(node_of(lax.rem(z + d, zs), x, c), f) for d in range(1, zs)]
    plane = [(dx, dc) for dx in range(xs) for dc in range(CORES) if dx or dc]
    partners += [(node_of(z, lax.rem(x + dx, xs), lax.rem(c + dc, CORES)), f) for dx, dc in plane]
    barrier = pltpu.get_barrier_semaphore()
    for to in partners:
        pl.semaphore_signal(barrier, inc=1, device_id=to, device_id_type=MESH)

    get_feats.wait()
    s.table[plan.blocks] = jnp.zeros((BLK, width), BF16)
    for i in range(plan.halo):
        block = s.table[idx[plan.send + i]]
        s.hsend[i] = jnp.concatenate([block[:half], block[half:]], axis=1)
    get_up.wait()

    def pack_up(p, _):
        s.upk[p] = jnp.concatenate([s.up[2 * p], s.up[2 * p + 1]], axis=1)
        return 0

    lax.fori_loop(0, plan.blocks // 2, pack_up, 0)
    for k in range(plan.stages):
        s.ur[k, f] = s.upk[k * nf + f]
    get_w.wait()

    pl.semaphore_wait(barrier, len(partners))

    far_first = sorted(range(1, nf), key=lambda d: -min(d, nf - d))
    halo_copies = []
    for i, d in enumerate(plan.offsets):
        to = (lax.rem(node - d + nn, nn), f)
        halo_copies.append(remote(s.hsend.at[i], s.hrecv.at[i], s.halo_s.at[i], s.halo_r.at[i], to))
    w_copies = [
        remote(s.wh.at[c, f], s.wh.at[c, f], s.w_s.at[d - 1], s.w_r.at[d - 1], (node, lax.rem(f + d, nf)))
        for d in far_first
    ]
    up_copies = []
    for k in range(plan.stages):
        for d in far_first:
            j = lax.rem(f + d, nf)
            up_copies.append(
                remote(s.upk.at[k * nf + j], s.ur.at[k, f], s.up_s.at[k, d - 1], s.up_r.at[k, d - 1], (node, j))
            )
    for copy in halo_copies + w_copies + up_copies:
        copy.start()

    s.fsum[0] = jnp.zeros((BLK, width), F32)
    s.hsum[0] = jnp.zeros((BLK, width), F32)
    get_tiles.wait()

    def forward_local(i, total):
        keep = idx[plan.fl_k + i].astype(F32)
        term = jnp.dot(s.tiles[idx[plan.fl_t + i]], s.table[idx[plan.fl_c + i]], preferred_element_type=F32)
        total = total * keep + term
        s.fsum[i + 1] = total
        return total

    zero = jnp.zeros((BLK, width), F32)
    lax.fori_loop(0, plan.local, forward_local, zero, unroll=8)

    for copy in w_copies:
        copy.wait()
    other = (node_of(z, x, 1 - c), f)
    w_swap = remote(s.wh.at[c], s.wh.at[c], s.wx.at[0], s.wx.at[1], other)
    w_swap.start()

    for copy in halo_copies:
        copy.wait()
    for i in range(plan.halo):
        block = s.hrecv[i]
        s.htable[i] = jnp.concatenate([block[:, :width], block[:, width:]], axis=0)

    def forward_halo(i, total):
        keep = idx[plan.fh_k + i].astype(F32)
        term = jnp.dot(s.tiles[idx[plan.fh_t + i]], s.htable[idx[plan.fh_s + i]], preferred_element_type=F32)
        total = total * keep + term
        s.hsum[i + 1] = total
        return total

    lax.fori_loop(0, plan.halo, forward_halo, zero, unroll=min(8, plan.halo))

    def summed(b):
        return (s.fsum[idx[plan.fl_end + b]] + s.hsum[idx[plan.fh_end + b]]).astype(BF16)

    agg_copies = []
    for k in range(plan.stages):
        stage_copies = []
        for d in far_first + [0]:
            j = lax.rem(f + d, nf)
            p = k * nf + j
            pair = jnp.concatenate([summed(2 * p), summed(2 * p + 1)], axis=1)
            if d == 0:
                s.ar[k, f] = pair
            else:
                s.apk[p] = pair
                copy = remote(s.apk.at[p], s.ar.at[k, f], s.ag_s.at[k, d - 1], s.ag_r.at[k, d - 1], (node, j))
                copy.start()
                stage_copies.append(copy)
        agg_copies.append(stage_copies)

    w_swap.wait()
    for j in range(nf):
        for h in range(CORES):
            rows = width // CORES
            s.wfull[pl.ds(j * width + h * rows, rows)] = s.wh[h, j]

    for copy in up_copies:
        copy.wait()

    def rows_of(ref, k):
        top = jnp.concatenate([ref[k, j][:, :width] for j in range(nf)], axis=1)
        bottom = jnp.concatenate([ref[k, j][:, width:] for j in range(nf)], axis=1)
        return jnp.concatenate([top, bottom], axis=0)

    grad_copies = []
    cols = plan.full // CORES
    for k in range(plan.stages):
        for copy in agg_copies[k]:
            copy.wait()
        s.xrows[...] = rows_of(s.ar, k)
        pre = jnp.dot(s.xrows[...], s.wfull[...], preferred_element_type=F32)
        sig = jax.nn.sigmoid(pre)
        upstream = rows_of(s.ur, k).astype(F32)
        s.gp[...] = (upstream * sig * (1.0 + pre * (1.0 - sig))).astype(BF16)
        grad = lax.dot_general(s.wfull[...], s.gp[...], (((1,), (1,)), ((), ())), preferred_element_type=F32)
        grad = grad.astype(BF16)
        for j in range(nf):
            s.gsend[k, j, 0] = grad[j * width : (j + 1) * width, :BLK]
            s.gsend[k, j, 1] = grad[j * width : (j + 1) * width, BLK:]
        for d in far_first:
            j = lax.rem(f + d, nf)
            copy = remote(
                s.gsend.at[k, j], s.grad.at[pl.ds(2 * (k * nf + f), 2)], s.gr_s.at[k, d - 1], s.gr_r.at[k, d - 1], (node, j)
            )
            copy.start()
            grad_copies.append(copy)
        s.grad[pl.ds(2 * (k * nf + f), 2)] = s.gsend[k, f]
        wg = lax.dot_general(s.xrows[...], s.gp[...], (((0,), (0,)), ((), ())), preferred_element_type=F32)
        for h in range(CORES):
            part = wg[:, h * cols : (h + 1) * cols].reshape(nf, width, cols)
            s.wg[h] = part if k == 0 else s.wg[h] + part

    wg_core = remote(s.wg.at[1 - c], s.wg_c, s.wc.at[0], s.wc.at[1], other)
    wg_core.start()

    s.grad[plan.blocks] = jnp.zeros((width, BLK), BF16)
    for copy in grad_copies:
        copy.wait()
    back_copies = []
    for i, d in enumerate(plan.offsets):
        term = jnp.dot(s.grad[idx[plan.bh_r + i]], s.tiles[idx[plan.bh_t + i]], preferred_element_type=F32)
        s.bsend[i] = term.astype(BF16)
        copy = remote(
            s.bsend.at[i], s.brecv.at[i], s.back_s.at[i], s.back_r.at[i], (lax.rem(node + d + nn, nn), f)
        )
        copy.start()
        back_copies.append(copy)

    wg_core.wait()
    rows = width // xs
    for at in range(xs):
        s.wg1[at] = s.wg[c, :, pl.ds(at * rows, rows), :] + s.wg_c[:, pl.ds(at * rows, rows), :]
    x_copies = []
    for d in range(1, xs):
        to_x = lax.rem(x + d, xs)
        copy = remote(s.wg1.at[to_x], s.wg_x.at[d - 1], s.wx_s.at[d - 1], s.wx_r.at[d - 1], (node_of(z, to_x, c), f))
        copy.start()
        x_copies.append(copy)

    s.bsum[0] = jnp.zeros((width, BLK), F32)
    s.rsum[0] = jnp.zeros((width, BLK), F32)

    def backward_local(i, total):
        keep = idx[plan.bl_k + i].astype(F32)
        term = jnp.dot(s.grad[idx[plan.bl_r + i]], s.tiles[idx[plan.bl_t + i]], preferred_element_type=F32)
        total = total * keep + term
        s.bsum[i + 1] = total
        return total

    zero_t = jnp.zeros((width, BLK), F32)
    lax.fori_loop(0, plan.local, backward_local, zero_t, unroll=8)

    for copy in x_copies:
        copy.wait()
    mine = s.wg1[x]
    for d in range(1, xs):
        mine = mine + s.wg_x[d - 1]
    s.wg2[...] = mine
    z_copies = []
    for d in range(1, zs):
        to_z = lax.rem(z + d, zs)
        copy = remote(s.wg2.at[to_z], s.wg_z.at[d - 1], s.wz_s.at[d - 1], s.wz_r.at[d - 1], (node_of(to_z, x, c), f))
        copy.start()
        z_copies.append(copy)

    for copy in back_copies:
        copy.wait()

    def returned(i, total):
        keep = idx[plan.r_k + i].astype(F32)
        total = total * keep + s.brecv[idx[plan.r_s + i]].astype(F32)
        s.rsum[i + 1] = total
        return total

    lax.fori_loop(0, plan.halo, returned, zero_t, unroll=min(4, plan.halo))

    for copy in z_copies:
        copy.wait()
    mine = s.wg2[z]
    for d in range(1, zs):
        mine = mine + s.wg_z[d - 1]
    s.wg3[...] = mine
    away = lax.rem(z - f + nf, nf)

    @pl.when(away != 0)
    def _():
        remote(s.wg3, s.wg_y.at[away - 1], s.wy_s.at[0], s.wy_r.at[away - 1], (node, z)).start()

    def finish(b, _):
        out_ref[b] = (s.bsum[idx[plan.bl_end + b]] + s.rsum[idx[plan.r_end + b]]).astype(BF16)
        return 0

    lax.fori_loop(0, plan.blocks, finish, 0, unroll=4)

    z_from = f
    z_away = lax.rem(z - z_from + zs, zs)

    @pl.when(away != 0)
    def _():
        remote(s.wg3, s.wg_y.at[away - 1], s.wy_s.at[0], s.wy_r.at[away - 1], (node, z)).wait_send()
        remote(
            s.wg4, s.wg4, s.wb_s.at[z_away - 1], s.wb_r.at[z_away - 1], (node_of(z_from, x, c), f)
        ).wait_recv()

    @pl.when(away == 0)
    def _():
        total = s.wg3[...]
        for d in range(1, nf):
            remote(s.wg3, s.wg_y.at[d - 1], s.wy_s.at[0], s.wy_r.at[d - 1], (node, lax.rem(f + d, nf))).wait_recv()
            total = total + s.wg_y[d - 1]
        s.wg4[...] = total
        copies = []
        for d in range(1, zs):
            to = (node_of(lax.rem(z + d, zs), x, c), f)
            copies.append(remote(s.wg4, s.wg4, s.wb_s.at[d - 1], s.wb_r.at[d - 1], to))
        for copy in copies:
            copy.start()
        for copy in copies:
            copy.wait_send()

    s.wg5[c, x] = s.wg4[...]
    last_copies = []
    for i, (dx, dc) in enumerate(plane):
        to = (node_of(z, lax.rem(x + dx, xs), lax.rem(c + dc, CORES)), f)
        copy = remote(s.wg4, s.wg5.at[c, x], s.wl_s.at[i], s.wl_r.at[i], to)
        copy.start()
        last_copies.append(copy)
    for copy in last_copies:
        copy.wait()
    for h in range(CORES):
        for at in range(xs):
            wout_ref[pl.ds(at * rows, rows), pl.ds(h * cols, cols)] = s.wg5[h, at]


class Scratch:
    pass


def scratch_of(plan):
    nf, ns, halo, blocks, width = plan.feats, plan.stages, plan.halo, plan.blocks, plan.width
    cols, rows = plan.full // CORES, width // plan.xs
    dma = pltpu.SemaphoreType.DMA
    vmem = pltpu.VMEM
    return {
        "table": vmem((blocks + 1, BLK, width), BF16),
        "up": vmem((blocks, BLK, width), BF16),
        "upk": vmem((blocks // 2, BLK, 2 * width), BF16),
        "ur": vmem((ns, nf, BLK, 2 * width), BF16),
        "wh": vmem((CORES, nf, width // CORES, plan.full), BF16),
        "wfull": vmem((plan.full, plan.full), BF16),
        "tiles": vmem((plan.tiles, BLK, BLK), BF16),
        "hsend": vmem((halo, BLK // 2, 2 * width), BF16),
        "hrecv": vmem((halo, BLK // 2, 2 * width), BF16),
        "htable": vmem((halo, BLK, width), BF16),
        "fsum": vmem((plan.local + 1, BLK, width), F32),
        "hsum": vmem((halo + 1, BLK, width), F32),
        "apk": vmem((blocks // 2, BLK, 2 * width), BF16),
        "ar": vmem((ns, nf, BLK, 2 * width), BF16),
        "xrows": vmem((2 * BLK, plan.full), BF16),
        "gp": vmem((2 * BLK, plan.full), BF16),
        "gsend": vmem((ns, nf, 2, width, BLK), BF16),
        "grad": vmem((blocks + 1, width, BLK), BF16),
        "wg": vmem((CORES, nf, width, cols), F32),
        "wg_c": vmem((nf, width, cols), F32),
        "wg1": vmem((plan.xs, nf, rows, cols), F32),
        "wg_x": vmem((plan.xs - 1, nf, rows, cols), F32),
        "wg2": vmem((nf, rows, cols), F32),
        "wg_z": vmem((plan.zs - 1, rows, cols), F32),
        "wg3": vmem((rows, cols), F32),
        "wg_y": vmem((nf - 1, rows, cols), F32),
        "wg4": vmem((rows, cols), F32),
        "wg5": vmem((CORES, plan.xs, rows, cols), F32),
        "bsend": vmem((halo, width, BLK), BF16),
        "brecv": vmem((halo, width, BLK), BF16),
        "bsum": vmem((plan.local + 1, width, BLK), F32),
        "rsum": vmem((halo + 1, width, BLK), F32),
        "get": dma((4,)),
        "halo_s": dma((halo,)), "halo_r": dma((halo,)),
        "w_s": dma((nf - 1,)), "w_r": dma((nf - 1,)),
        "wx": dma((2,)),
        "up_s": dma((ns, nf - 1)), "up_r": dma((ns, nf - 1)),
        "ag_s": dma((ns, nf - 1)), "ag_r": dma((ns, nf - 1)),
        "gr_s": dma((ns, nf - 1)), "gr_r": dma((ns, nf - 1)),
        "back_s": dma((halo,)), "back_r": dma((halo,)),
        "wc": dma((2,)),
        "wx_s": dma((plan.xs - 1,)), "wx_r": dma((plan.xs - 1,)),
        "wz_s": dma((plan.zs - 1,)), "wz_r": dma((plan.zs - 1,)),
        "wy_s": dma((1,)), "wy_r": dma((nf - 1,)),
        "wb_s": dma((plan.zs - 1,)), "wb_r": dma((plan.zs - 1,)),
        "wl_s": dma((CORES * plan.xs - 1,)), "wl_r": dma((CORES * plan.xs - 1,)),
    }


def local(offsets_of, x_chips, features, weight, tile_row, tile_col, tile_count, send_blocks, tile_values, upstream):
    rows_dev, width = features.shape
    blocks = rows_dev // BLK
    nodes, feats = lax.axis_size("node"), lax.axis_size("feat")
    plan = Plan(blocks, width, tile_row.shape[0], feats, nodes, offsets_of(nodes), x_chips)
    idx = index_lists(plan, tile_row, tile_col, tile_count, send_blocks)
    scratch = scratch_of(plan)
    names = list(scratch)

    def body(idx, feats_hbm, up_hbm, w_hbm, tiles_hbm, out_ref, wout_ref, *refs):
        s = Scratch()
        for name, ref in zip(names, refs):
            setattr(s, name, ref)
        kernel(plan, idx, feats_hbm, up_hbm, w_hbm, tiles_hbm, out_ref, wout_ref, s)

    anywhere = pl.BlockSpec(memory_space=pl.ANY)
    in_vmem = pl.BlockSpec(memory_space=pltpu.VMEM)
    grad_t, weight_sum = pl.pallas_call(
        body,
        out_shape=(
            jax.ShapeDtypeStruct((blocks, width, BLK), BF16),
            jax.ShapeDtypeStruct((width, plan.full), F32),
        ),
        in_specs=[pl.BlockSpec(memory_space=pltpu.SMEM), anywhere, anywhere, anywhere, anywhere],
        out_specs=(in_vmem, in_vmem),
        scratch_shapes=[scratch[name] for name in names],
        compiler_params=pltpu.CompilerParams(
            collective_id=0, has_side_effects=True, vmem_limit_bytes=52 * 1024 * 1024
        ),
    )(idx, features.reshape(blocks, BLK, width), upstream.reshape(blocks, BLK, width), weight, tile_values)
    features_grad = jnp.swapaxes(grad_t, 1, 2).reshape(rows_dev, width)
    return features_grad, weight_sum / math.sqrt(rows_dev * nodes)


def build(mesh, offsets_of, x_chips):
    in_specs = (
        P("node", "feat"),
        P("feat", None),
        P("node"),
        P("node"),
        P("node"),
        P("node", None, None),
        P("node", None, None),
        P("node", "feat"),
    )
    out_specs = (P("node", "feat"), P("feat", None))
    return jax.shard_map(
        functools.partial(local, offsets_of, x_chips), mesh=mesh, in_specs=in_specs, out_specs=out_specs, check_vma=False
    )


def solution(mesh):
    return build(mesh, halo_offsets, X_CHIPS)
```

```python
import functools
import math

import jax
import jax.numpy as jnp
from jax import lax
from jax.experimental import pallas as pl
from jax.experimental.pallas import tpu as pltpu
from jax.sharding import PartitionSpec as P

MESH = pl.DeviceIdType.MESH
F32 = jnp.float32
BF16 = jnp.bfloat16
BLK = 128
CORES = 2
X_CHIPS = 4


def halo_offsets(node_count):
    near = [step for d in range(1, 8) for step in (d, -d)]
    return near + [8, 32]


class Plan:
    def __init__(self, blocks, width, tiles, feats, nodes, offsets, x_chips):
        self.blocks, self.width, self.tiles = blocks, width, tiles
        self.feats, self.nodes, self.offsets = feats, nodes, offsets
        self.halo = len(offsets)
        self.local = tiles - self.halo
        self.full = width * feats
        self.stages = blocks // (2 * feats)
        self.xs = x_chips
        self.zs = nodes // (CORES * x_chips)


LANES = 128
BITS = 7
MASK = (1 << BITS) - 1
(FL_T, FL_C, FL_K, FL_END, FH_T, FH_S, FH_K, FH_END, BH_T, BH_R, BL_T, BL_R, BL_K, BL_END, R_S, R_K, R_END) = range(17)
LISTS = 24


def iota(dim, rows=LANES):
    return lax.broadcasted_iota(jnp.int32, (rows, LANES), dim)


def as_columns(vector):
    return jnp.broadcast_to(vector, (LANES, LANES)).T


def count(where):
    return jnp.sum(jnp.where(where, 1, 0), axis=0, keepdims=True)


def pick(one_hot, columns):
    return jnp.sum(jnp.where(one_hot, columns, 0), axis=0, keepdims=True)


def in_order(group, first, second):
    lane, sub = iota(1), iota(0)
    down = as_columns(group)
    smaller = count(down < group)
    rank = smaller + count(jnp.logical_and(down == group, sub < lane))
    follows = jnp.where(rank > smaller, 1, 0)
    packed = as_columns(rank + (first << BITS) + (second << (2 * BITS)) + (follows << (3 * BITS)))
    got = pick((packed & MASK) == lane, packed >> BITS)
    end = jnp.where(count(down == lane) > 0, count(down <= lane), 0)
    return got & MASK, (got >> BITS) & MASK, got >> (2 * BITS), end


def write_lists(plan, node, live, row_ref, col_ref, send_ref, line, lists):
    n = plan.nodes
    lane = iota(1, 1)
    line[...] = jnp.zeros_like(line)
    line[0:1, 0 : plan.tiles] = row_ref[...]
    line[1:2, 0 : plan.tiles] = col_ref[...]
    line[2:3, 0:n] = send_ref[...]
    row, col, sends = line[0:1, :], line[1:2, :], line[2:3, :]
    alive = lane < live
    local = jnp.logical_and(alive, col < plan.blocks)
    row_in, col_in = jnp.where(local, row, plan.blocks), jnp.where(local, col, plan.blocks)
    fl_t, fl_c, fl_k, fl_end = in_order(row_in, lane, col_in)
    bl_t, bl_r, bl_k, bl_end = in_order(col_in, lane, row_in)

    reads, serves = jnp.full((1, LANES), -1, jnp.int32), jnp.full((1, LANES), -1, jnp.int32)
    for i, d in enumerate(plan.offsets):
        reads = jnp.where(lane == i, plan.blocks + lax.rem(node + d + n, n), reads)
        serves = jnp.where(lane == i, lax.rem(node - d + n, n), serves)
    packed = as_columns(jnp.where(alive, col + (row << BITS), 0))
    got = pick((packed & MASK) == reads, (packed >> BITS) + (iota(0) << BITS))
    bh_t, bh_r = got >> BITS, got & MASK
    target = pick(iota(0) == serves, as_columns(sends))
    used = lane < plan.halo
    fh_t, fh_s, fh_k, fh_end = in_order(jnp.where(used, bh_r, plan.blocks), bh_t, lane)
    r_s, _, r_k, r_end = in_order(jnp.where(used, target, plan.blocks), lane, lane)
    rows = [fl_t, fl_c, fl_k, fl_end, fh_t, fh_s, fh_k, fh_end, bh_t, bh_r, bl_t, bl_r, bl_k, bl_end, r_s, r_k, r_end]
    lists[...] = jnp.zeros_like(lists)
    for i, vector in enumerate(rows):
        lists[i : i + 1, :] = vector


def kernel(plan, count_ref, send_sm, row_ref, col_ref, send_ref, feats_hbm, up_hbm, w_hbm, tiles_hbm, out_ref, wout_ref, s):
    nf, nn, width = plan.feats, plan.nodes, plan.width
    zs, xs = plan.zs, plan.xs
    rows, cols = width // xs, plan.full // CORES
    pair = 2 * BLK
    node, f = lax.axis_index("node"), lax.axis_index("feat")
    c = lax.rem(node, CORES)
    x = lax.rem(node // CORES, xs)
    z = node // (CORES * xs)
    idx = s.idx

    def node_of(z_at, x_at, c_at):
        return (z_at * xs + x_at) * CORES + c_at

    def remote(src, dst, send_sem, recv_sem, to):
        return pltpu.make_async_remote_copy(
            src_ref=src, dst_ref=dst, send_sem=send_sem, recv_sem=recv_sem, device_id=to, device_id_type=MESH
        )

    def up_pair(p):
        return up_hbm.at[:, pl.ds(pl.multiple_of(p * pair, pair), pair)]

    get_feats = pltpu.make_async_copy(feats_hbm, s.feats, s.get.at[0])
    get_w = pltpu.make_async_copy(
        w_hbm.at[pl.ds(x * rows, rows), pl.ds(pl.multiple_of(c * cols, cols), cols)], s.wq.at[c, x, f], s.get.at[1]
    )
    get_tiles = pltpu.make_async_copy(tiles_hbm, s.tiles, s.get.at[2])
    get_up = [pltpu.make_async_copy(up_pair(k * nf + f), s.ur.at[k, f], s.get.at[3 + k]) for k in range(plan.stages)]
    for copy in [get_feats, get_w, get_tiles] + get_up:
        copy.start()

    near = sorted({d % nn for d in plan.offsets} | {-d % nn for d in plan.offsets})
    plane = [(dx, dc) for dx in range(xs) for dc in range(CORES) if dx or dc]
    partners = [(node_of(lax.rem(z + d, zs), x, c), f) for d in range(1, zs)]
    partners += [(lax.rem(node + d, nn), f) for d in near]
    partners += [(node_of(z, lax.rem(x + dx, xs), lax.rem(c + dc, CORES)), f) for dx, dc in plane]
    partners += [(node, lax.rem(f + d, nf)) for d in range(1, nf)]
    barrier = pltpu.get_barrier_semaphore()
    for to in partners:
        pl.semaphore_signal(barrier, inc=1, device_id=to, device_id_type=MESH)

    get_w.wait()
    pl.semaphore_wait(barrier, len(partners))

    far_first = sorted(range(1, nf), key=lambda d: -min(d, nf - d))
    w_copies = [
        remote(s.wq.at[c, x, f], s.wq.at[c, x, f], s.w_s.at[d - 1], s.w_r.at[d - 1], (node, lax.rem(f + d, nf)))
        for d in far_first
    ]
    up_copies = []
    for k in range(plan.stages):
        stage_copies = []
        for d in far_first:
            j = lax.rem(f + d, nf)
            stage_copies.append(
                remote(up_pair(k * nf + j), s.ur.at[k, f], s.up_s.at[k, d - 1], s.up_r.at[k, d - 1], (node, j))
            )
        up_copies.append(stage_copies)
    for copy in w_copies + up_copies[0]:
        copy.start()
    get_feats.wait()
    for b in range(plan.blocks):
        s.table[b] = s.feats[:, b * BLK : (b + 1) * BLK]
    s.table[plan.blocks] = jnp.zeros((width, BLK), BF16)
    halo_copies = []
    for i, d in enumerate(plan.offsets):
        to = lax.rem(node - d + nn, nn)
        s.hsend[i] = s.table[send_sm[0, to]]
        copy = remote(s.hsend.at[i], s.hrecv.at[i], s.halo_s.at[i], s.halo_r.at[i], (to, f))
        copy.start()
        halo_copies.append(copy)
    for copy in sum(up_copies[1:], []):
        copy.start()

    write_lists(plan, node, count_ref[0], row_ref, col_ref, send_ref, s.line, s.lists)
    put_lists = pltpu.make_async_copy(s.lists, s.idx, s.get.at[3 + plan.stages])
    put_lists.start()
    zero = jnp.zeros((width, BLK), F32)
    for ref in (s.fsum, s.hsum, s.bsum, s.rsum):
        ref[0] = zero
    s.grad[plan.blocks] = jnp.zeros((width, BLK), BF16)

    for copy in w_copies:
        copy.wait()
    wx_copies = []
    for d in range(1, xs):
        to = (node_of(z, lax.rem(x + d, xs), c), f)
        wx_copies.append(remote(s.wq.at[c, x], s.wq.at[c, x], s.wqx_s.at[d - 1], s.wqx_r.at[d - 1], to))
    for copy in wx_copies:
        copy.start()

    put_lists.wait()
    get_tiles.wait()

    def forward_local(i, total):
        keep = idx[FL_K, i].astype(F32)
        term = lax.dot_general(
            s.table[idx[FL_C, i]], s.tiles[idx[FL_T, i]], (((1,), (1,)), ((), ())), preferred_element_type=F32
        )
        total = total * keep + term
        s.fsum[i + 1] = total
        return total

    lax.fori_loop(0, plan.local, forward_local, zero, unroll=16)

    for copy in halo_copies:
        copy.wait()

    def forward_halo(i, total):
        keep = idx[FH_K, i].astype(F32)
        term = lax.dot_general(
            s.hrecv[idx[FH_S, i]], s.tiles[idx[FH_T, i]], (((1,), (1,)), ((), ())), preferred_element_type=F32
        )
        total = total * keep + term
        s.hsum[i + 1] = total
        return total

    lax.fori_loop(0, plan.halo, forward_halo, zero, unroll=plan.halo)

    def summed(b):
        return (s.fsum[idx[FL_END, b]] + s.hsum[idx[FH_END, b]]).astype(BF16)

    agg_copies = []
    for k in range(plan.stages):
        stage_copies = []
        for d in far_first + [0]:
            j = lax.rem(f + d, nf)
            p = k * nf + j
            into = s.apk.at[p] if d else s.ar.at[k, f]
            into[:, 0:BLK] = summed(2 * p)
            into[:, BLK:pair] = summed(2 * p + 1)
            if d:
                copy = remote(s.apk.at[p], s.ar.at[k, f], s.ag_s.at[k, d - 1], s.ag_r.at[k, d - 1], (node, j))
                copy.start()
                stage_copies.append(copy)
        agg_copies.append(stage_copies)

    for copy in wx_copies:
        copy.wait()
    other = (node_of(z, x, 1 - c), f)
    w_swap = remote(s.wq.at[c], s.wq.at[c], s.wsw.at[0], s.wsw.at[1], other)
    w_swap.start()
    w_swap.wait()
    for j in range(nf):
        for at in range(xs):
            for h in range(CORES):
                s.wfull[pl.ds(j * width + at * rows, rows), pl.ds(h * cols, cols)] = s.wq[h, at, j]
    s.wt[...] = s.wfull[...].T

    grad_copies = []
    for k in range(plan.stages):
        get_up[k].wait()
        for copy in up_copies[k] + agg_copies[k]:
            copy.wait()
        agg = s.ar[k].reshape(plan.full, pair)
        pre = jnp.dot(s.wt[...], agg, preferred_element_type=F32)
        sig = jax.nn.sigmoid(pre)
        upstream = s.ur[k].reshape(plan.full, pair).astype(F32)
        s.gp[...] = (upstream * sig * (1.0 + pre * (1.0 - sig))).astype(BF16)

        def weight_part():
            wg = lax.dot_general(agg, s.gp[...], (((1,), (1,)), ((), ())), preferred_element_type=F32)
            for h in range(CORES):
                part = wg[:, h * cols : (h + 1) * cols].reshape(nf, width, cols)
                s.wg[h] = part if k == 0 else s.wg[h] + part

        last = k == plan.stages - 1
        if last:
            weight_part()
            wg_core = remote(s.wg.at[1 - c], s.wg_c, s.wc.at[0], s.wc.at[1], other)
            wg_core.start()
        grad = jnp.dot(s.wfull[...], s.gp[...], preferred_element_type=F32).astype(BF16)
        for j in range(nf):
            for h in range(2):
                s.gsend[k, j, h] = grad[j * width : (j + 1) * width, h * BLK : (h + 1) * BLK]
        for d in far_first:
            j = lax.rem(f + d, nf)
            copy = remote(
                s.gsend.at[k, j], s.grad.at[pl.ds(2 * (k * nf + f), 2)], s.gr_s.at[k, d - 1], s.gr_r.at[k, d - 1], (node, j)
            )
            copy.start()
            grad_copies.append(copy)
        s.grad[pl.ds(2 * (k * nf + f), 2)] = s.gsend[k, f]
        if not last:
            weight_part()

    wg_core.wait()
    x_copies = []
    for d in list(range(1, xs)) + [0]:
        to_x = lax.rem(x + d, xs)
        at = pl.ds(pl.multiple_of(to_x * rows, rows), rows)
        part = s.wg[c, :, at, :] + s.wg_c[:, at, :]
        if d:
            s.wg1[d - 1] = part.astype(BF16)
            to = (node_of(z, to_x, c), f)
            copy = remote(s.wg1.at[d - 1], s.wg_x.at[d - 1], s.wx_s.at[d - 1], s.wx_r.at[d - 1], to)
            copy.start()
            x_copies.append(copy)
        else:
            s.wg2[...] = part
    for copy in x_copies:
        copy.wait()
    s.wg2[...] = sum([s.wg_x[d].astype(F32) for d in range(xs - 1)], s.wg2[...])
    z_copies = []
    for d in range(1, zs):
        to_z = lax.rem(z + d, zs)
        copy = remote(s.wg2.at[to_z], s.wg_z.at[d - 1], s.wz_s.at[d - 1], s.wz_r.at[d - 1], (node_of(to_z, x, c), f))
        copy.start()
        z_copies.append(copy)

    for copy in grad_copies:
        copy.wait()
    back_copies = []
    for i, d in enumerate(plan.offsets):
        term = jnp.dot(s.grad[idx[BH_R, i]], s.tiles[idx[BH_T, i]], preferred_element_type=F32)
        s.bsend[i] = term.astype(BF16)
        copy = remote(
            s.bsend.at[i], s.brecv.at[i], s.back_s.at[i], s.back_r.at[i], (lax.rem(node + d + nn, nn), f)
        )
        copy.start()
        back_copies.append(copy)

    for copy in z_copies:
        copy.wait()
    s.wg3[...] = sum([s.wg_z[d] for d in range(zs - 1)], s.wg2[z])
    away = lax.rem(z - f + nf, nf)

    @pl.when(away != 0)
    def _():
        remote(s.wg3, s.wg_y.at[away - 1], s.wy_s.at[0], s.wy_r.at[away - 1], (node, z)).start()

    def backward_local(i, total):
        keep = idx[BL_K, i].astype(F32)
        term = jnp.dot(s.grad[idx[BL_R, i]], s.tiles[idx[BL_T, i]], preferred_element_type=F32)
        total = total * keep + term
        s.bsum[i + 1] = total
        return total

    lax.fori_loop(0, plan.local, backward_local, zero, unroll=16)

    @pl.when(away != 0)
    def _():
        remote(s.wg3, s.wg_y.at[away - 1], s.wy_s.at[0], s.wy_r.at[away - 1], (node, z)).wait_send()

    @pl.when(away == 0)
    def _():
        total = s.wg3[...]
        for d in range(1, nf):
            remote(s.wg3, s.wg_y.at[d - 1], s.wy_s.at[0], s.wy_r.at[d - 1], (node, lax.rem(f + d, nf))).wait_recv()
            total = total + s.wg_y[d - 1]
        s.wg4[...] = total
        for d in range(1, zs):
            to = (node_of(lax.rem(z + d, zs), x, c), f)
            remote(s.wg4, s.wg4, s.wb_s.at[d - 1], s.wb_r.at[d - 1], to).start()

    for copy in back_copies:
        copy.wait()

    def returned(i, total):
        keep = idx[R_K, i].astype(F32)
        total = total * keep + s.brecv[idx[R_S, i]].astype(F32)
        s.rsum[i + 1] = total
        return total

    lax.fori_loop(0, plan.halo, returned, zero, unroll=plan.halo)

    @pl.when(away != 0)
    def _():
        remote(s.wg4, s.wg4, s.wb_s.at[away - 1], s.wb_r.at[away - 1], (node_of(f, x, c), f)).wait_recv()

    @pl.when(away == 0)
    def _():
        for d in range(1, zs):
            to = (node_of(lax.rem(z + d, zs), x, c), f)
            remote(s.wg4, s.wg4, s.wb_s.at[d - 1], s.wb_r.at[d - 1], to).wait_send()

    s.wg5[c, x] = s.wg4[...]
    last_copies = []
    for i, (dx, dc) in enumerate(plane):
        to = (node_of(z, lax.rem(x + dx, xs), lax.rem(c + dc, CORES)), f)
        copy = remote(s.wg4, s.wg5.at[c, x], s.wl_s.at[i], s.wl_r.at[i], to)
        copy.start()
        last_copies.append(copy)
    for b in range(plan.blocks):
        out_ref[:, b * BLK : (b + 1) * BLK] = (s.bsum[idx[BL_END, b]] + s.rsum[idx[R_END, b]]).astype(BF16)

    for copy in last_copies:
        copy.wait()
    for h in range(CORES):
        for at in range(xs):
            wout_ref[pl.ds(at * rows, rows), pl.ds(h * cols, cols)] = s.wg5[h, at]


class Scratch:
    pass


def scratch_of(plan):
    nf, ns, halo, blocks, width = plan.feats, plan.stages, plan.halo, plan.blocks, plan.width
    cols, rows = plan.full // CORES, width // plan.xs
    dma = pltpu.SemaphoreType.DMA
    vmem = pltpu.VMEM
    return {
        "feats": vmem((width, blocks * BLK), BF16),
        "table": vmem((blocks + 1, width, BLK), BF16),
        "ur": vmem((ns, nf, width, 2 * BLK), BF16),
        "wq": vmem((CORES, plan.xs, nf, rows, cols), BF16),
        "wfull": vmem((plan.full, plan.full), BF16),
        "wt": vmem((plan.full, plan.full), BF16),
        "tiles": vmem((plan.tiles, BLK, BLK), BF16),
        "hsend": vmem((halo, width, BLK), BF16),
        "hrecv": vmem((halo, width, BLK), BF16),
        "fsum": vmem((plan.local + 1, width, BLK), F32),
        "hsum": vmem((halo + 1, width, BLK), F32),
        "apk": vmem((blocks // 2, width, 2 * BLK), BF16),
        "ar": vmem((ns, nf, width, 2 * BLK), BF16),
        "gp": vmem((plan.full, 2 * BLK), BF16),
        "gsend": vmem((ns, nf, 2, width, BLK), BF16),
        "grad": vmem((blocks + 1, width, BLK), BF16),
        "line": vmem((8, LANES), jnp.int32),
        "lists": vmem((LISTS, LANES), jnp.int32),
        "idx": pltpu.SMEM((LISTS, LANES), jnp.int32),
        "wg": vmem((CORES, nf, width, cols), F32),
        "wg_c": vmem((nf, width, cols), F32),
        "wg1": vmem((plan.xs - 1, nf, rows, cols), BF16),
        "wg_x": vmem((plan.xs - 1, nf, rows, cols), BF16),
        "wg2": vmem((nf, rows, cols), F32),
        "wg_z": vmem((plan.zs - 1, rows, cols), F32),
        "wg3": vmem((rows, cols), F32),
        "wg_y": vmem((nf - 1, rows, cols), F32),
        "wg4": vmem((rows, cols), F32),
        "wg5": vmem((CORES, plan.xs, rows, cols), F32),
        "bsend": vmem((halo, width, BLK), BF16),
        "brecv": vmem((halo, width, BLK), BF16),
        "bsum": vmem((plan.local + 1, width, BLK), F32),
        "rsum": vmem((halo + 1, width, BLK), F32),
        "get": dma((4 + ns,)),
        "halo_s": dma((halo,)), "halo_r": dma((halo,)),
        "w_s": dma((nf - 1,)), "w_r": dma((nf - 1,)),
        "wqx_s": dma((plan.xs - 1,)), "wqx_r": dma((plan.xs - 1,)),
        "wsw": dma((2,)),
        "up_s": dma((ns, nf - 1)), "up_r": dma((ns, nf - 1)),
        "ag_s": dma((ns, nf - 1)), "ag_r": dma((ns, nf - 1)),
        "gr_s": dma((ns, nf - 1)), "gr_r": dma((ns, nf - 1)),
        "back_s": dma((halo,)), "back_r": dma((halo,)),
        "wc": dma((2,)),
        "wx_s": dma((plan.xs - 1,)), "wx_r": dma((plan.xs - 1,)),
        "wz_s": dma((plan.zs - 1,)), "wz_r": dma((plan.zs - 1,)),
        "wy_s": dma((1,)), "wy_r": dma((nf - 1,)),
        "wb_s": dma((plan.zs - 1,)), "wb_r": dma((plan.zs - 1,)),
        "wl_s": dma((CORES * plan.xs - 1,)), "wl_r": dma((CORES * plan.xs - 1,)),
    }


def local(offsets_of, x_chips, features, weight, tile_row, tile_col, tile_count, send_blocks, tile_values, upstream):
    rows_dev, width = features.shape
    blocks = rows_dev // BLK
    nodes, feats = lax.axis_size("node"), lax.axis_size("feat")
    plan = Plan(blocks, width, tile_row.shape[0], feats, nodes, offsets_of(nodes), x_chips)
    scratch = scratch_of(plan)
    names = list(scratch)
    given = 9

    def body(*refs):
        s = Scratch()
        for name, ref in zip(names, refs[given + 2 :]):
            setattr(s, name, ref)
        kernel(plan, *refs[: given + 2], s)

    anywhere = pl.BlockSpec(memory_space=pltpu.HBM)
    in_vmem = pl.BlockSpec(memory_space=pltpu.VMEM)
    in_smem = pl.BlockSpec(memory_space=pltpu.SMEM)
    sends = send_blocks.reshape(1, nodes)
    grad_t, weight_sum = pl.pallas_call(
        body,
        out_shape=(
            pltpu.VMEM((width, rows_dev), BF16),
            pltpu.VMEM((width, plan.full), F32),
        ),
        in_specs=[in_smem, in_smem, in_vmem, in_vmem, in_vmem, anywhere, anywhere, anywhere, anywhere],
        out_specs=(in_vmem, in_vmem),
        scratch_shapes=[scratch[name] for name in names],
        compiler_params=pltpu.CompilerParams(
            collective_id=0, has_side_effects=True, vmem_limit_bytes=62 * 1024 * 1024
        ),
    )(
        tile_count, sends, tile_row.reshape(1, -1), tile_col.reshape(1, -1), sends,
        features.T, upstream.T, weight, tile_values,
    )
    return grad_t.T, weight_sum / math.sqrt(rows_dev * nodes)


def build(mesh, offsets_of, x_chips):
    in_specs = (
        P("node", "feat"),
        P("feat", None),
        P("node"),
        P("node"),
        P("node"),
        P("node", None, None),
        P("node", None, None),
        P("node", "feat"),
    )
    out_specs = (P("node", "feat"), P("feat", None))
    return jax.shard_map(
        functools.partial(local, offsets_of, x_chips), mesh=mesh, in_specs=in_specs, out_specs=out_specs, check_vma=False
    )


def solution(mesh):
    return build(mesh, halo_offsets, X_CHIPS)
```

```python
import functools
import math

import jax
import jax.numpy as jnp
from jax import lax
from jax.experimental import pallas as pl
from jax.experimental.pallas import tpu as pltpu
from jax.sharding import PartitionSpec as P

MESH = pl.DeviceIdType.MESH
F32 = jnp.float32
BF16 = jnp.bfloat16
BLK = 128
CORES = 2
X_CHIPS = 4


def halo_offsets(node_count):
    near = [step for d in range(1, 8) for step in (d, -d)]
    return near + [8, 32]


class Plan:
    def __init__(self, blocks, width, tiles, feats, nodes, offsets, x_chips):
        self.blocks, self.width, self.tiles = blocks, width, tiles
        self.feats, self.nodes, self.offsets = feats, nodes, offsets
        self.halo = len(offsets)
        self.local = tiles - self.halo
        self.full = width * feats
        self.stages = blocks // (2 * feats)
        self.xs = x_chips
        self.zs = nodes // (CORES * x_chips)


LANES = 128
BITS = 7
MASK = (1 << BITS) - 1
(FL_T, FL_C, FL_K, FL_END, FH_T, FH_S, FH_K, FH_END, BH_T, BH_R, BL_T, BL_R, BL_K, BL_END, R_S, R_K, R_END) = range(17)
LISTS = 24


def iota(dim, rows=LANES):
    return lax.broadcasted_iota(jnp.int32, (rows, LANES), dim)


def as_columns(vector):
    return jnp.broadcast_to(vector, (LANES, LANES)).T


def count(where):
    return jnp.sum(jnp.where(where, 1, 0), axis=0, keepdims=True)


def pick(one_hot, columns):
    return jnp.sum(jnp.where(one_hot, columns, 0), axis=0, keepdims=True)


def in_order(group, first, second):
    lane, sub = iota(1), iota(0)
    down = as_columns(group)
    smaller = count(down < group)
    rank = smaller + count(jnp.logical_and(down == group, sub < lane))
    follows = jnp.where(rank > smaller, 1, 0)
    packed = as_columns(rank + (first << BITS) + (second << (2 * BITS)) + (follows << (3 * BITS)))
    got = pick((packed & MASK) == lane, packed >> BITS)
    end = jnp.where(count(down == lane) > 0, count(down <= lane), 0)
    return got & MASK, (got >> BITS) & MASK, got >> (2 * BITS), end


def write_lists(plan, node, live, row_ref, col_ref, send_ref, line, lists):
    n = plan.nodes
    lane = iota(1, 1)
    line[...] = jnp.zeros_like(line)
    line[0:1, 0 : plan.tiles] = row_ref[...]
    line[1:2, 0 : plan.tiles] = col_ref[...]
    line[2:3, 0:n] = send_ref[...]
    row, col, sends = line[0:1, :], line[1:2, :], line[2:3, :]
    alive = lane < live
    local = jnp.logical_and(alive, col < plan.blocks)
    row_in, col_in = jnp.where(local, row, plan.blocks), jnp.where(local, col, plan.blocks)
    fl_t, fl_c, fl_k, fl_end = in_order(row_in, lane, col_in)
    bl_t, bl_r, bl_k, bl_end = in_order(col_in, lane, row_in)

    reads, serves = jnp.full((1, LANES), -1, jnp.int32), jnp.full((1, LANES), -1, jnp.int32)
    for i, d in enumerate(plan.offsets):
        reads = jnp.where(lane == i, plan.blocks + lax.rem(node + d + n, n), reads)
        serves = jnp.where(lane == i, lax.rem(node - d + n, n), serves)
    packed = as_columns(jnp.where(alive, col + (row << BITS), 0))
    got = pick((packed & MASK) == reads, (packed >> BITS) + (iota(0) << BITS))
    bh_t, bh_r = got >> BITS, got & MASK
    target = pick(iota(0) == serves, as_columns(sends))
    used = lane < plan.halo
    fh_t, fh_s, fh_k, fh_end = in_order(jnp.where(used, bh_r, plan.blocks), bh_t, lane)
    r_s, _, r_k, r_end = in_order(jnp.where(used, target, plan.blocks), lane, lane)
    rows = [fl_t, fl_c, fl_k, fl_end, fh_t, fh_s, fh_k, fh_end, bh_t, bh_r, bl_t, bl_r, bl_k, bl_end, r_s, r_k, r_end]
    lists[...] = jnp.zeros_like(lists)
    for i, vector in enumerate(rows):
        lists[i : i + 1, :] = vector


def kernel(plan, count_hbm, send_hbm, row_hbm, col_hbm, feats_hbm, up_hbm, w_hbm, tiles_hbm, out_ref, wout_ref, s):
    nf, nn, width = plan.feats, plan.nodes, plan.width
    zs, xs = plan.zs, plan.xs
    rows, cols = width // xs, plan.full // CORES
    pair = 2 * BLK
    node, f = lax.axis_index("node"), lax.axis_index("feat")
    c = lax.rem(node, CORES)
    x = lax.rem(node // CORES, xs)
    z = node // (CORES * xs)
    idx = s.idx

    def node_of(z_at, x_at, c_at):
        return (z_at * xs + x_at) * CORES + c_at

    def remote(src, dst, send_sem, recv_sem, to):
        return pltpu.make_async_remote_copy(
            src_ref=src, dst_ref=dst, send_sem=send_sem, recv_sem=recv_sem, device_id=to, device_id_type=MESH
        )

    def up_pair(p):
        return up_hbm.at[:, pl.ds(pl.multiple_of(p * pair, pair), pair)]

    get_feats = pltpu.make_async_copy(feats_hbm, s.feats, s.get.at[0])
    get_w = pltpu.make_async_copy(
        w_hbm.at[pl.ds(x * rows, rows), pl.ds(pl.multiple_of(c * cols, cols), cols)], s.wq.at[c, x, f], s.get.at[1]
    )
    get_tiles = pltpu.make_async_copy(tiles_hbm, s.tiles, s.get.at[2])
    get_up = [pltpu.make_async_copy(up_pair(k * nf + f), s.ur.at[k, f], s.get.at[3 + k]) for k in range(plan.stages)]
    get_send = pltpu.make_async_copy(send_hbm, s.send_sm, s.get_small.at[0])
    get_lines = [
        pltpu.make_async_copy(src, dst, s.get_small.at[1 + i])
        for i, (src, dst) in enumerate(
            [(send_hbm, s.send_v), (row_hbm, s.row_v), (col_hbm, s.col_v), (count_hbm, s.count_v)]
        )
    ]
    for copy in [get_w, get_send, get_feats, get_tiles] + get_up + get_lines:
        copy.start()

    near = sorted({d % nn for d in plan.offsets} | {-d % nn for d in plan.offsets})
    plane = [(dx, dc) for dx in range(xs) for dc in range(CORES) if dx or dc]
    partners = [(node_of(lax.rem(z + d, zs), x, c), f) for d in range(1, zs)]
    partners += [(lax.rem(node + d, nn), f) for d in near]
    partners += [(node_of(z, lax.rem(x + dx, xs), lax.rem(c + dc, CORES)), f) for dx, dc in plane]
    partners += [(node, lax.rem(f + d, nf)) for d in range(1, nf)]
    barrier = pltpu.get_barrier_semaphore()
    for to in partners:
        pl.semaphore_signal(barrier, inc=1, device_id=to, device_id_type=MESH)

    get_w.wait()
    pl.semaphore_wait(barrier, len(partners))

    far_first = sorted(range(1, nf), key=lambda d: -min(d, nf - d))
    w_copies = [
        remote(s.wq.at[c, x, f], s.wq.at[c, x, f], s.w_s.at[d - 1], s.w_r.at[d - 1], (node, lax.rem(f + d, nf)))
        for d in far_first
    ]
    up_copies = []
    for k in range(plan.stages):
        stage_copies = []
        for d in far_first:
            j = lax.rem(f + d, nf)
            stage_copies.append(
                remote(up_pair(k * nf + j), s.ur.at[k, f], s.up_s.at[k, d - 1], s.up_r.at[k, d - 1], (node, j))
            )
        up_copies.append(stage_copies)
    for copy in w_copies + up_copies[0]:
        copy.start()
    get_feats.wait()
    get_send.wait()
    for b in range(plan.blocks):
        s.table[b] = s.feats[:, b * BLK : (b + 1) * BLK]
    s.table[plan.blocks] = jnp.zeros((width, BLK), BF16)
    halo_copies = []
    for i, d in enumerate(plan.offsets):
        to = lax.rem(node - d + nn, nn)
        s.hsend[i] = s.table[s.send_sm[0, to]]
        copy = remote(s.hsend.at[i], s.hrecv.at[i], s.halo_s.at[i], s.halo_r.at[i], (to, f))
        copy.start()
        halo_copies.append(copy)
    for copy in sum(up_copies[1:], []):
        copy.start()

    for copy in get_lines:
        copy.wait()
    write_lists(plan, node, s.count_v[...], s.row_v, s.col_v, s.send_v, s.line, s.lists)
    put_lists = pltpu.make_async_copy(s.lists, s.idx, s.get.at[3 + plan.stages])
    put_lists.start()
    zero = jnp.zeros((width, BLK), F32)
    for ref in (s.fsum, s.hsum, s.bsum, s.rsum):
        ref[0] = zero
    s.grad[plan.blocks] = jnp.zeros((width, BLK), BF16)

    for copy in w_copies:
        copy.wait()
    wx_copies = []
    for d in range(1, xs):
        to = (node_of(z, lax.rem(x + d, xs), c), f)
        wx_copies.append(remote(s.wq.at[c, x], s.wq.at[c, x], s.wqx_s.at[d - 1], s.wqx_r.at[d - 1], to))
    for copy in wx_copies:
        copy.start()

    put_lists.wait()
    get_tiles.wait()

    def forward_local(i, total):
        keep = idx[FL_K, i].astype(F32)
        term = lax.dot_general(
            s.table[idx[FL_C, i]], s.tiles[idx[FL_T, i]], (((1,), (1,)), ((), ())), preferred_element_type=F32
        )
        total = total * keep + term
        s.fsum[i + 1] = total
        return total

    lax.fori_loop(0, plan.local, forward_local, zero, unroll=16)

    for copy in halo_copies:
        copy.wait()

    def forward_halo(i, total):
        keep = idx[FH_K, i].astype(F32)
        term = lax.dot_general(
            s.hrecv[idx[FH_S, i]], s.tiles[idx[FH_T, i]], (((1,), (1,)), ((), ())), preferred_element_type=F32
        )
        total = total * keep + term
        s.hsum[i + 1] = total
        return total

    lax.fori_loop(0, plan.halo, forward_halo, zero, unroll=plan.halo)

    def summed(b):
        return (s.fsum[idx[FL_END, b]] + s.hsum[idx[FH_END, b]]).astype(BF16)

    agg_copies = []
    for k in range(plan.stages):
        stage_copies = []
        for d in far_first + [0]:
            j = lax.rem(f + d, nf)
            p = k * nf + j
            into = s.apk.at[p] if d else s.ar.at[k, f]
            into[:, 0:BLK] = summed(2 * p)
            into[:, BLK:pair] = summed(2 * p + 1)
            if d:
                copy = remote(s.apk.at[p], s.ar.at[k, f], s.ag_s.at[k, d - 1], s.ag_r.at[k, d - 1], (node, j))
                copy.start()
                stage_copies.append(copy)
        agg_copies.append(stage_copies)

    for copy in wx_copies:
        copy.wait()
    other = (node_of(z, x, 1 - c), f)
    w_swap = remote(s.wq.at[c], s.wq.at[c], s.wsw.at[0], s.wsw.at[1], other)
    w_swap.start()
    w_swap.wait()
    for j in range(nf):
        for at in range(xs):
            for h in range(CORES):
                s.wfull[pl.ds(j * width + at * rows, rows), pl.ds(h * cols, cols)] = s.wq[h, at, j]
    s.wt[...] = s.wfull[...].T

    grad_copies = []

    def send_grad(k):
        for d in far_first:
            j = lax.rem(f + d, nf)
            copy = remote(
                s.gsend.at[k, j], s.grad.at[pl.ds(2 * (k * nf + f), 2)], s.gr_s.at[k, d - 1], s.gr_r.at[k, d - 1], (node, j)
            )
            copy.start()
            grad_copies.append(copy)

    for k in range(plan.stages):
        get_up[k].wait()
        for copy in up_copies[k] + agg_copies[k]:
            copy.wait()
        if k:
            send_grad(k - 1)
        agg = s.ar[k].reshape(plan.full, pair)
        pre = jnp.dot(s.wt[...], agg, preferred_element_type=F32)
        sig = jax.nn.sigmoid(pre)
        upstream = s.ur[k].reshape(plan.full, pair).astype(F32)
        s.gp[...] = (upstream * sig * (1.0 + pre * (1.0 - sig))).astype(BF16)

        def weight_part():
            wg = lax.dot_general(agg, s.gp[...], (((1,), (1,)), ((), ())), preferred_element_type=F32)
            for h in range(CORES):
                part = wg[:, h * cols : (h + 1) * cols].reshape(nf, width, cols)
                s.wg[h] = part if k == 0 else s.wg[h] + part

        last = k == plan.stages - 1
        if last:
            weight_part()
            s.wg0[...] = s.wg[1 - c].astype(BF16)
            wg_core = remote(s.wg0, s.wg_c, s.wc.at[0], s.wc.at[1], other)
            wg_core.start()
        grad = jnp.dot(s.wfull[...], s.gp[...], preferred_element_type=F32).astype(BF16)
        for j in range(nf):
            for h in range(2):
                s.gsend[k, j, h] = grad[j * width : (j + 1) * width, h * BLK : (h + 1) * BLK]
        if last:
            send_grad(k)
        s.grad[pl.ds(2 * (k * nf + f), 2)] = s.gsend[k, f]
        if not last:
            weight_part()

    wg_core.wait()
    x_copies = []
    for d in list(range(1, xs)) + [0]:
        to_x = lax.rem(x + d, xs)
        at = pl.ds(pl.multiple_of(to_x * rows, rows), rows)
        part = s.wg[c, :, at, :] + s.wg_c[:, at, :].astype(F32)
        if d:
            s.wg1[d - 1] = part.astype(BF16)
            to = (node_of(z, to_x, c), f)
            copy = remote(s.wg1.at[d - 1], s.wg_x.at[d - 1], s.wx_s.at[d - 1], s.wx_r.at[d - 1], to)
            copy.start()
            x_copies.append(copy)
        else:
            s.wg2[...] = part
    for copy in x_copies:
        copy.wait()
    s.wg2[...] = sum([s.wg_x[d].astype(F32) for d in range(xs - 1)], s.wg2[...])
    s.wg2b[...] = s.wg2[...].astype(BF16)
    y_copies = []
    for d in far_first:
        j = lax.rem(f + d, nf)
        copy = remote(s.wg2b.at[j], s.wg_y.at[d - 1], s.wy_s.at[d - 1], s.wy_r.at[d - 1], (node, j))
        copy.start()
        y_copies.append(copy)
    for copy in y_copies:
        copy.wait()
    s.wg3[...] = sum([s.wg_y[d].astype(F32) for d in range(nf - 1)], s.wg2[f]).astype(BF16)
    s.wg_z[z] = s.wg3[...]
    z_copies = []
    for d in range(1, zs):
        to = (node_of(lax.rem(z + d, zs), x, c), f)
        copy = remote(s.wg3, s.wg_z.at[z], s.wz_s.at[d - 1], s.wz_r.at[d - 1], to)
        copy.start()
        z_copies.append(copy)

    for copy in grad_copies:
        copy.wait()
    back_copies = []
    for i, d in enumerate(plan.offsets):
        term = jnp.dot(s.grad[idx[BH_R, i]], s.tiles[idx[BH_T, i]], preferred_element_type=F32)
        s.bsend[i] = term.astype(BF16)
        copy = remote(
            s.bsend.at[i], s.brecv.at[i], s.back_s.at[i], s.back_r.at[i], (lax.rem(node + d + nn, nn), f)
        )
        copy.start()
        back_copies.append(copy)

    def backward_local(i, total):
        keep = idx[BL_K, i].astype(F32)
        term = jnp.dot(s.grad[idx[BL_R, i]], s.tiles[idx[BL_T, i]], preferred_element_type=F32)
        total = total * keep + term
        s.bsum[i + 1] = total
        return total

    middle = plan.local // 2
    total = lax.fori_loop(0, middle, backward_local, zero, unroll=16)

    for copy in z_copies:
        copy.wait()
    s.wg4[...] = sum([s.wg_z[at].astype(F32) for at in range(1, zs)], s.wg_z[0].astype(F32))
    s.wg5[c, x] = s.wg4[...]
    last_copies = []
    for i, (dx, dc) in enumerate(plane):
        to = (node_of(z, lax.rem(x + dx, xs), lax.rem(c + dc, CORES)), f)
        copy = remote(s.wg4, s.wg5.at[c, x], s.wl_s.at[i], s.wl_r.at[i], to)
        copy.start()
        last_copies.append(copy)

    lax.fori_loop(middle, plan.local, backward_local, total, unroll=16)

    for copy in back_copies:
        copy.wait()

    def returned(i, total):
        keep = idx[R_K, i].astype(F32)
        total = total * keep + s.brecv[idx[R_S, i]].astype(F32)
        s.rsum[i + 1] = total
        return total

    lax.fori_loop(0, plan.halo, returned, zero, unroll=plan.halo)

    for b in range(plan.blocks):
        out_ref[:, b * BLK : (b + 1) * BLK] = (s.bsum[idx[BL_END, b]] + s.rsum[idx[R_END, b]]).astype(BF16)

    for copy in last_copies:
        copy.wait()
    for h in range(CORES):
        for at in range(xs):
            wout_ref[pl.ds(at * rows, rows), pl.ds(h * cols, cols)] = s.wg5[h, at]


class Scratch:
    pass


def scratch_of(plan):
    nf, ns, halo, blocks, width = plan.feats, plan.stages, plan.halo, plan.blocks, plan.width
    cols, rows = plan.full // CORES, width // plan.xs
    dma = pltpu.SemaphoreType.DMA
    vmem = pltpu.VMEM
    return {
        "feats": vmem((width, blocks * BLK), BF16),
        "table": vmem((blocks + 1, width, BLK), BF16),
        "ur": vmem((ns, nf, width, 2 * BLK), BF16),
        "wq": vmem((CORES, plan.xs, nf, rows, cols), BF16),
        "wfull": vmem((plan.full, plan.full), BF16),
        "wt": vmem((plan.full, plan.full), BF16),
        "tiles": vmem((plan.tiles, BLK, BLK), BF16),
        "hsend": vmem((halo, width, BLK), BF16),
        "hrecv": vmem((halo, width, BLK), BF16),
        "fsum": vmem((plan.local + 1, width, BLK), F32),
        "hsum": vmem((halo + 1, width, BLK), F32),
        "apk": vmem((blocks // 2, width, 2 * BLK), BF16),
        "ar": vmem((ns, nf, width, 2 * BLK), BF16),
        "gp": vmem((plan.full, 2 * BLK), BF16),
        "gsend": vmem((ns, nf, 2, width, BLK), BF16),
        "grad": vmem((blocks + 1, width, BLK), BF16),
        "send_sm": pltpu.SMEM((1, plan.nodes), jnp.int32),
        "send_v": vmem((1, plan.nodes), jnp.int32),
        "row_v": vmem((1, plan.tiles), jnp.int32),
        "col_v": vmem((1, plan.tiles), jnp.int32),
        "count_v": vmem((1, 1), jnp.int32),
        "get_small": dma((5,)),
        "line": vmem((8, LANES), jnp.int32),
        "lists": vmem((LISTS, LANES), jnp.int32),
        "idx": pltpu.SMEM((LISTS, LANES), jnp.int32),
        "wg": vmem((CORES, nf, width, cols), F32),
        "wg0": vmem((nf, width, cols), BF16),
        "wg_c": vmem((nf, width, cols), BF16),
        "wg1": vmem((plan.xs - 1, nf, rows, cols), BF16),
        "wg_x": vmem((plan.xs - 1, nf, rows, cols), BF16),
        "wg2": vmem((nf, rows, cols), F32),
        "wg2b": vmem((nf, rows, cols), BF16),
        "wg_z": vmem((plan.zs, rows, cols), BF16),
        "wg3": vmem((rows, cols), BF16),
        "wg_y": vmem((nf - 1, rows, cols), BF16),
        "wg4": vmem((rows, cols), F32),
        "wg5": vmem((CORES, plan.xs, rows, cols), F32),
        "bsend": vmem((halo, width, BLK), BF16),
        "brecv": vmem((halo, width, BLK), BF16),
        "bsum": vmem((plan.local + 1, width, BLK), F32),
        "rsum": vmem((halo + 1, width, BLK), F32),
        "get": dma((4 + ns,)),
        "halo_s": dma((halo,)), "halo_r": dma((halo,)),
        "w_s": dma((nf - 1,)), "w_r": dma((nf - 1,)),
        "wqx_s": dma((plan.xs - 1,)), "wqx_r": dma((plan.xs - 1,)),
        "wsw": dma((2,)),
        "up_s": dma((ns, nf - 1)), "up_r": dma((ns, nf - 1)),
        "ag_s": dma((ns, nf - 1)), "ag_r": dma((ns, nf - 1)),
        "gr_s": dma((ns, nf - 1)), "gr_r": dma((ns, nf - 1)),
        "back_s": dma((halo,)), "back_r": dma((halo,)),
        "wc": dma((2,)),
        "wx_s": dma((plan.xs - 1,)), "wx_r": dma((plan.xs - 1,)),
        "wz_s": dma((plan.zs - 1,)), "wz_r": dma((plan.zs - 1,)),
        "wy_s": dma((nf - 1,)), "wy_r": dma((nf - 1,)),
        "wl_s": dma((CORES * plan.xs - 1,)), "wl_r": dma((CORES * plan.xs - 1,)),
    }


def local(offsets_of, x_chips, features, weight, tile_row, tile_col, tile_count, send_blocks, tile_values, upstream):
    rows_dev, width = features.shape
    blocks = rows_dev // BLK
    nodes, feats = lax.axis_size("node"), lax.axis_size("feat")
    plan = Plan(blocks, width, tile_row.shape[0], feats, nodes, offsets_of(nodes), x_chips)
    scratch = scratch_of(plan)
    names = list(scratch)
    given = 8

    def body(*refs):
        s = Scratch()
        for name, ref in zip(names, refs[given + 2 :]):
            setattr(s, name, ref)
        kernel(plan, *refs[: given + 2], s)

    anywhere = pl.BlockSpec(memory_space=pltpu.HBM)
    in_vmem = pl.BlockSpec(memory_space=pltpu.VMEM)
    grad_t, weight_sum = pl.pallas_call(
        body,
        out_shape=(
            pltpu.VMEM((width, rows_dev), BF16),
            pltpu.VMEM((width, plan.full), F32),
        ),
        in_specs=[anywhere] * given,
        out_specs=(in_vmem, in_vmem),
        scratch_shapes=[scratch[name] for name in names],
        compiler_params=pltpu.CompilerParams(
            collective_id=0, has_side_effects=True, vmem_limit_bytes=62 * 1024 * 1024
        ),
    )(
        tile_count.reshape(1, 1), send_blocks.reshape(1, nodes), tile_row.reshape(1, -1), tile_col.reshape(1, -1),
        features.T, upstream.T, weight, tile_values,
    )
    return grad_t.T, weight_sum / math.sqrt(rows_dev * nodes)


def build(mesh, offsets_of, x_chips):
    in_specs = (
        P("node", "feat"),
        P("feat", None),
        P("node"),
        P("node"),
        P("node"),
        P("node", None, None),
        P("node", None, None),
        P("node", "feat"),
    )
    out_specs = (P("node", "feat"), P("feat", None))
    return jax.shard_map(
        functools.partial(local, offsets_of, x_chips), mesh=mesh, in_specs=in_specs, out_specs=out_specs, check_vma=False
    )


def solution(mesh):
    return build(mesh, halo_offsets, X_CHIPS)
```

```python
import functools
import math

import jax
import jax.numpy as jnp
from jax import lax
from jax.experimental import pallas as pl
from jax.experimental.pallas import tpu as pltpu
from jax.sharding import PartitionSpec as P

MESH = pl.DeviceIdType.MESH
F32 = jnp.float32
BF16 = jnp.bfloat16
BLK = 128
CORES = 2
X_CHIPS = 4


def halo_offsets(node_count):
    near = [step for d in range(1, 8) for step in (d, -d)]
    return near + [8, 32]


class Plan:
    def __init__(self, blocks, width, tiles, feats, nodes, offsets, x_chips):
        self.blocks, self.width, self.tiles = blocks, width, tiles
        self.feats, self.nodes, self.offsets = feats, nodes, offsets
        self.halo = len(offsets)
        self.local = tiles - self.halo
        self.full = width * feats
        self.stages = blocks // (2 * feats)
        self.xs = x_chips
        self.zs = nodes // (CORES * x_chips)


LANES = 128
BITS = 7
MASK = (1 << BITS) - 1
(FL_T, FL_C, FL_K, FL_END, FH_T, FH_S, FH_K, FH_END, BH_T, BH_R, BL_T, BL_R, BL_K, BL_END, R_S, R_K, R_END) = range(17)
LISTS = 24
HELD = 7


def iota(dim, rows=LANES):
    return lax.broadcasted_iota(jnp.int32, (rows, LANES), dim)


def as_columns(vector):
    return jnp.broadcast_to(vector, (LANES, LANES)).T


def count(where):
    return jnp.sum(jnp.where(where, 1, 0), axis=0, keepdims=True)


def pick(one_hot, columns):
    return jnp.sum(jnp.where(one_hot, columns, 0), axis=0, keepdims=True)


def in_order(group, first, second):
    lane, sub = iota(1), iota(0)
    down = as_columns(group)
    smaller = count(down < group)
    rank = smaller + count(jnp.logical_and(down == group, sub < lane))
    follows = jnp.where(rank > smaller, 1, 0)
    packed = as_columns(rank + (first << BITS) + (second << (2 * BITS)) + (follows << (3 * BITS)))
    got = pick((packed & MASK) == lane, packed >> BITS)
    end = jnp.where(count(down == lane) > 0, count(down <= lane), 0)
    return got & MASK, (got >> BITS) & MASK, got >> (2 * BITS), end


def write_order(plan, node, live, row_ref, col_ref, send_ref, line, first):
    n = plan.nodes
    lane = iota(1, 1)
    line[...] = jnp.zeros_like(line)
    line[0:1, 0 : plan.tiles] = row_ref[...]
    line[1:2, 0 : plan.tiles] = col_ref[...]
    line[2:3, 0:n] = send_ref[...]
    row, col = line[0:1, :], line[1:2, :]
    alive = lane < live
    reads = jnp.full((1, LANES), -1, jnp.int32)
    for i, d in enumerate(plan.offsets):
        reads = jnp.where(lane == i, plan.blocks + lax.rem(node + d + n, n), reads)
    packed = as_columns(jnp.where(alive, col + (row << BITS), 0))
    got = pick((packed & MASK) == reads, (packed >> BITS) + (iota(0) << BITS))
    bh_t, bh_r = got >> BITS, got & MASK
    rows_used = as_columns(jnp.where(lane < plan.halo, bh_r, plan.blocks))
    group = jnp.where(lane < plan.blocks, jnp.where(count(rows_used == lane) > 0, 0, 1), 2)
    down = as_columns(group)
    place = count(down < group) + count(jnp.logical_and(down == group, iota(0) < iota(1)))
    place_down = as_columns(place)
    order = pick(place_down == lane, iota(0))
    first[...] = jnp.zeros_like(first)
    first[0:1, :] = order
    return bh_t, bh_r, place_down


def write_lists(plan, node, live, order, line, lists):
    n = plan.nodes
    lane = iota(1, 1)
    bh_t, bh_r, place_down = order
    row, col, sends = line[0:1, :], line[1:2, :], line[2:3, :]
    local = jnp.logical_and(lane < live, col < plan.blocks)
    row_in, col_in = jnp.where(local, row, plan.blocks), jnp.where(local, col, plan.blocks)
    fl_t, fl_c, fl_k, fl_end = in_order(row_in, lane, col_in)
    bl_t, bl_r, bl_k, bl_end = in_order(col_in, lane, pick(iota(0) == row_in, place_down))
    serves = jnp.full((1, LANES), -1, jnp.int32)
    for i, d in enumerate(plan.offsets):
        serves = jnp.where(lane == i, lax.rem(node - d + n, n), serves)
    target = pick(iota(0) == serves, as_columns(sends))
    used = lane < plan.halo
    fh_t, fh_s, fh_k, fh_end = in_order(jnp.where(used, bh_r, plan.blocks), bh_t, lane)
    r_s, _, r_k, r_end = in_order(jnp.where(used, target, plan.blocks), lane, lane)
    bh_p = pick(iota(0) == bh_r, place_down)
    rows = [fl_t, fl_c, fl_k, fl_end, fh_t, fh_s, fh_k, fh_end, bh_t, bh_p, bl_t, bl_r, bl_k, bl_end, r_s, r_k, r_end]
    lists[...] = jnp.zeros_like(lists)
    for i, vector in enumerate(rows):
        lists[i : i + 1, :] = vector


def kernel(plan, count_hbm, send_hbm, row_hbm, col_hbm, feats_hbm, up_hbm, w_hbm, tiles_hbm, out_ref, wout_ref, s):
    nf, nn, width = plan.feats, plan.nodes, plan.width
    zs, xs = plan.zs, plan.xs
    rows, cols = width // xs, plan.full // CORES
    pair = 2 * BLK
    node, f = lax.axis_index("node"), lax.axis_index("feat")
    c = lax.rem(node, CORES)
    x = lax.rem(node // CORES, xs)
    z = node // (CORES * xs)
    idx = s.idx

    def node_of(z_at, x_at, c_at):
        return (z_at * xs + x_at) * CORES + c_at

    def remote(src, dst, send_sem, recv_sem, to):
        return pltpu.make_async_remote_copy(
            src_ref=src, dst_ref=dst, send_sem=send_sem, recv_sem=recv_sem, device_id=to, device_id_type=MESH
        )

    get_feats = pltpu.make_async_copy(feats_hbm, s.feats, s.get.at[0])
    get_w = pltpu.make_async_copy(
        w_hbm.at[pl.ds(x * rows, rows), pl.ds(pl.multiple_of(c * cols, cols), cols)], s.wq.at[c, x, f], s.get.at[1]
    )
    get_tiles = pltpu.make_async_copy(tiles_hbm, s.tiles, s.get.at[2])
    get_up = pltpu.make_async_copy(up_hbm, s.up, s.get.at[3])
    get_send = pltpu.make_async_copy(send_hbm, s.send_sm, s.get_small.at[0])
    get_lines = [
        pltpu.make_async_copy(src, dst, s.get_small.at[1 + i])
        for i, (src, dst) in enumerate(
            [(send_hbm, s.send_v), (row_hbm, s.row_v), (col_hbm, s.col_v), (count_hbm, s.count_v)]
        )
    ]
    for copy in [get_w, get_send] + get_lines + [get_feats, get_up, get_tiles]:
        copy.start()

    near = sorted({d % nn for d in plan.offsets} | {-d % nn for d in plan.offsets})
    plane = [(dx, dc) for dx in range(xs) for dc in range(CORES) if dx or dc]
    partners = [(node_of(lax.rem(z + d, zs), x, c), f) for d in range(1, zs)]
    partners += [(lax.rem(node + d, nn), f) for d in near]
    partners += [(node_of(z, lax.rem(x + dx, xs), lax.rem(c + dc, CORES)), f) for dx, dc in plane]
    partners += [(node, lax.rem(f + d, nf)) for d in range(1, nf)]
    barrier = pltpu.get_barrier_semaphore()
    for to in partners:
        pl.semaphore_signal(barrier, inc=1, device_id=to, device_id_type=MESH)

    get_w.wait()
    pl.semaphore_wait(barrier, len(partners))

    far_first = sorted(range(1, nf), key=lambda d: -min(d, nf - d))
    w_copies = [
        remote(s.wq.at[c, x, f], s.wq.at[c, x, f], s.w_s.at[d - 1], s.w_r.at[d - 1], (node, lax.rem(f + d, nf)))
        for d in far_first
    ]
    for copy in w_copies:
        copy.start()

    for copy in get_lines:
        copy.wait()
    live = s.count_v[...]
    order = write_order(plan, node, live, s.row_v, s.col_v, s.send_v, s.line, s.order_v)
    put_order = pltpu.make_async_copy(s.order_v, s.order, s.get.at[4])
    put_order.start()

    get_feats.wait()
    get_send.wait()
    for b in range(plan.blocks):
        s.table[b] = s.feats[:, b * BLK : (b + 1) * BLK]
    s.table[plan.blocks] = jnp.zeros((width, BLK), BF16)
    halo_copies = []
    for i, d in enumerate(plan.offsets):
        to = lax.rem(node - d + nn, nn)
        s.hsend[i] = s.table[s.send_sm[0, to]]
        copy = remote(s.hsend.at[i], s.hrecv.at[i], s.halo_s.at[i], s.halo_r.at[i], (to, f))
        copy.start()
        halo_copies.append(copy)

    get_up.wait()
    for b in range(plan.blocks):
        s.uptable[b] = s.up[:, b * BLK : (b + 1) * BLK]
    put_order.wait()
    up_copies = []
    for k in range(plan.stages):
        stage_copies = []
        for d in far_first + [0]:
            j = lax.rem(f + d, nf)
            p = k * nf + j
            into = s.upk.at[p] if d else s.ur.at[k, f]
            into[:, 0:BLK] = s.uptable[s.order[0, 2 * p]]
            into[:, BLK:pair] = s.uptable[s.order[0, 2 * p + 1]]
            if d:
                copy = remote(s.upk.at[p], s.ur.at[k, f], s.up_s.at[k, d - 1], s.up_r.at[k, d - 1], (node, j))
                copy.start()
                stage_copies.append(copy)
        up_copies.append(stage_copies)

    write_lists(plan, node, live, order, s.line, s.lists)
    put_lists = pltpu.make_async_copy(s.lists, s.idx, s.get.at[5])
    put_lists.start()
    zero = jnp.zeros((width, BLK), F32)
    for ref in (s.fsum, s.hsum, s.bsum, s.rsum):
        ref[0] = zero
    s.grad[plan.blocks] = jnp.zeros((width, BLK), BF16)

    for copy in w_copies:
        copy.wait()
    wx_copies = []
    for d in range(1, xs):
        to = (node_of(z, lax.rem(x + d, xs), c), f)
        wx_copies.append(remote(s.wq.at[c, x], s.wq.at[c, x], s.wqx_s.at[d - 1], s.wqx_r.at[d - 1], to))
    for copy in wx_copies:
        copy.start()

    put_lists.wait()
    get_tiles.wait()

    def forward_local(i, total):
        keep = idx[FL_K, i].astype(F32)
        term = lax.dot_general(
            s.table[idx[FL_C, i]], s.tiles[idx[FL_T, i]], (((1,), (1,)), ((), ())), preferred_element_type=F32
        )
        total = total * keep + term
        s.fsum[i + 1] = total
        return total

    lax.fori_loop(0, plan.local, forward_local, zero, unroll=16)

    for copy in halo_copies:
        copy.wait()

    def forward_halo(i, total):
        keep = idx[FH_K, i].astype(F32)
        term = lax.dot_general(
            s.hrecv[idx[FH_S, i]], s.tiles[idx[FH_T, i]], (((1,), (1,)), ((), ())), preferred_element_type=F32
        )
        total = total * keep + term
        s.hsum[i + 1] = total
        return total

    lax.fori_loop(0, plan.halo, forward_halo, zero, unroll=plan.halo)

    def summed(at):
        b = s.order[0, at]
        return (s.fsum[idx[FL_END, b]] + s.hsum[idx[FH_END, b]]).astype(BF16)

    agg_copies = []
    for k in range(plan.stages):
        stage_copies = []
        for d in far_first + [0]:
            j = lax.rem(f + d, nf)
            p = k * nf + j
            into = s.apk.at[p] if d else s.ar.at[k, f]
            into[:, 0:BLK] = summed(2 * p)
            into[:, BLK:pair] = summed(2 * p + 1)
            if d:
                copy = remote(s.apk.at[p], s.ar.at[k, f], s.ag_s.at[k, d - 1], s.ag_r.at[k, d - 1], (node, j))
                copy.start()
                stage_copies.append(copy)
        agg_copies.append(stage_copies)

    for copy in wx_copies:
        copy.wait()
    other = (node_of(z, x, 1 - c), f)
    w_swap = remote(s.wq.at[c], s.wq.at[c], s.wsw.at[0], s.wsw.at[1], other)
    w_swap.start()
    w_swap.wait()
    for j in range(nf):
        for at in range(xs):
            for h in range(CORES):
                s.wfull[pl.ds(j * width + at * rows, rows), pl.ds(h * cols, cols)] = s.wq[h, at, j]
    s.wt[...] = s.wfull[...].T

    grad_copies = [[] for _ in range(plan.stages)]

    def send_grad(k, distances):
        for d in distances:
            j = lax.rem(f + d, nf)
            into = s.first.at[pl.ds(2 * f, 2)] if k == 0 else s.grad.at[pl.ds(2 * (k * nf + f), 2)]
            copy = remote(s.gsend.at[k, j], into, s.gr_s.at[k, d - 1], s.gr_r.at[k, d - 1], (node, j))
            copy.start()
            grad_copies[k].append(copy)

    for k in range(plan.stages):
        for copy in up_copies[k] + agg_copies[k]:
            copy.wait()
        if k:
            send_grad(k - 1, far_first)
        agg = s.ar[k].reshape(plan.full, pair)
        pre = jnp.dot(s.wt[...], agg, preferred_element_type=F32)
        sig = jax.nn.sigmoid(pre)
        upstream = s.ur[k].reshape(plan.full, pair).astype(F32)
        s.gp[...] = (upstream * sig * (1.0 + pre * (1.0 - sig))).astype(BF16)

        def weight_part(h):
            columns = s.gp[pl.ds(pl.multiple_of(h * cols, cols), cols)]
            wg = lax.dot_general(agg, columns, (((1,), (1,)), ((), ())), preferred_element_type=F32)
            return wg.reshape(nf, width, cols) + (s.wg[h] if k else 0.0)

        last = k == plan.stages - 1
        if last:
            s.wg0[...] = weight_part(1 - c).astype(BF16)
            wg_core = remote(s.wg0, s.wg_c, s.wc.at[0], s.wc.at[1], other)
            wg_core.start()
        grad = jnp.dot(s.wfull[...], s.gp[...], preferred_element_type=F32).astype(BF16)
        for j in range(nf):
            for h in range(2):
                s.gsend[k, j, h] = grad[j * width : (j + 1) * width, h * BLK : (h + 1) * BLK]
        if last:
            send_grad(k, far_first[HELD:])
        into = s.first.at[pl.ds(2 * f, 2)] if k == 0 else s.grad.at[pl.ds(2 * (k * nf + f), 2)]
        into[...] = s.gsend[k, f]
        if last:
            s.wg[c] = weight_part(c)
        else:
            for h in range(CORES):
                s.wg[h] = weight_part(h)

    wg_core.wait()
    x_copies = []
    for d in list(range(1, xs)) + [0]:
        to_x = lax.rem(x + d, xs)
        at = pl.ds(pl.multiple_of(to_x * rows, rows), rows)
        part = s.wg[c, :, at, :] + s.wg_c[:, at, :].astype(F32)
        if d:
            s.wg1[d - 1] = part.astype(BF16)
            to = (node_of(z, to_x, c), f)
            copy = remote(s.wg1.at[d - 1], s.wg_x.at[d - 1], s.wx_s.at[d - 1], s.wx_r.at[d - 1], to)
            copy.start()
            x_copies.append(copy)
        else:
            s.wg2[...] = part
    for copy in x_copies:
        copy.wait()
    s.wg2[...] = sum([s.wg_x[d].astype(F32) for d in range(xs - 1)], s.wg2[...])
    s.wg2b[...] = s.wg2[...].astype(BF16)
    y_copies = []
    for d in far_first:
        j = lax.rem(f + d, nf)
        copy = remote(s.wg2b.at[j], s.wg_y.at[d - 1], s.wy_s.at[d - 1], s.wy_r.at[d - 1], (node, j))
        copy.start()
        y_copies.append(copy)
    send_grad(plan.stages - 1, far_first[:HELD])
    for copy in grad_copies[0]:
        copy.wait()
    back_copies = []
    for i, d in enumerate(plan.offsets):
        term = jnp.dot(s.first[idx[BH_R, i]], s.tiles[idx[BH_T, i]], preferred_element_type=F32)
        s.bsend[i] = term.astype(BF16)
        copy = remote(
            s.bsend.at[i], s.brecv.at[i], s.back_s.at[i], s.back_r.at[i], (lax.rem(node + d + nn, nn), f)
        )
        copy.start()
        back_copies.append(copy)
    s.grad[pl.ds(0, 2 * nf)] = s.first[...]

    for copy in y_copies:
        copy.wait()
    s.wg3[...] = sum([s.wg_y[d].astype(F32) for d in range(nf - 1)], s.wg2[f]).astype(BF16)
    s.wg_z[z] = s.wg3[...]
    z_copies = []
    for d in range(1, zs):
        to = (node_of(lax.rem(z + d, zs), x, c), f)
        copy = remote(s.wg3, s.wg_z.at[z], s.wz_s.at[d - 1], s.wz_r.at[d - 1], to)
        copy.start()
        z_copies.append(copy)

    for copy in z_copies:
        copy.wait()
    s.wg4[...] = sum([s.wg_z[at].astype(F32) for at in range(1, zs)], s.wg_z[0].astype(F32))
    s.wg5[c, x] = s.wg4[...]
    last_copies = []
    for i, (dx, dc) in enumerate(plane):
        to = (node_of(z, lax.rem(x + dx, xs), lax.rem(c + dc, CORES)), f)
        copy = remote(s.wg4, s.wg5.at[c, x], s.wl_s.at[i], s.wl_r.at[i], to)
        copy.start()
        last_copies.append(copy)

    for copy in sum(grad_copies[1:], []):
        copy.wait()

    def backward_local(i, total):
        keep = idx[BL_K, i].astype(F32)
        term = jnp.dot(s.grad[idx[BL_R, i]], s.tiles[idx[BL_T, i]], preferred_element_type=F32)
        total = total * keep + term
        s.bsum[i + 1] = total
        return total

    lax.fori_loop(0, plan.local, backward_local, zero, unroll=16)

    for copy in back_copies:
        copy.wait()

    def returned(i, total):
        keep = idx[R_K, i].astype(F32)
        total = total * keep + s.brecv[idx[R_S, i]].astype(F32)
        s.rsum[i + 1] = total
        return total

    lax.fori_loop(0, plan.halo, returned, zero, unroll=plan.halo)

    for b in range(plan.blocks):
        out_ref[:, b * BLK : (b + 1) * BLK] = (s.bsum[idx[BL_END, b]] + s.rsum[idx[R_END, b]]).astype(BF16)

    for copy in last_copies:
        copy.wait()
    for h in range(CORES):
        for at in range(xs):
            wout_ref[pl.ds(at * rows, rows), pl.ds(h * cols, cols)] = s.wg5[h, at]


class Scratch:
    pass


def scratch_of(plan):
    nf, ns, halo, blocks, width = plan.feats, plan.stages, plan.halo, plan.blocks, plan.width
    cols, rows = plan.full // CORES, width // plan.xs
    dma = pltpu.SemaphoreType.DMA
    vmem = pltpu.VMEM
    return {
        "feats": vmem((width, blocks * BLK), BF16),
        "table": vmem((blocks + 1, width, BLK), BF16),
        "up": vmem((width, blocks * BLK), BF16),
        "uptable": vmem((blocks, width, BLK), BF16),
        "upk": vmem((blocks // 2, width, 2 * BLK), BF16),
        "ur": vmem((ns, nf, width, 2 * BLK), BF16),
        "wq": vmem((CORES, plan.xs, nf, rows, cols), BF16),
        "wfull": vmem((plan.full, plan.full), BF16),
        "wt": vmem((plan.full, plan.full), BF16),
        "tiles": vmem((plan.tiles, BLK, BLK), BF16),
        "hsend": vmem((halo, width, BLK), BF16),
        "hrecv": vmem((halo, width, BLK), BF16),
        "fsum": vmem((plan.local + 1, width, BLK), F32),
        "hsum": vmem((halo + 1, width, BLK), F32),
        "apk": vmem((blocks // 2, width, 2 * BLK), BF16),
        "ar": vmem((ns, nf, width, 2 * BLK), BF16),
        "gp": vmem((plan.full, 2 * BLK), BF16),
        "gsend": vmem((ns, nf, 2, width, BLK), BF16),
        "first": vmem((2 * nf, width, BLK), BF16),
        "grad": vmem((blocks + 1, width, BLK), BF16),
        "send_sm": pltpu.SMEM((1, plan.nodes), jnp.int32),
        "send_v": vmem((1, plan.nodes), jnp.int32),
        "row_v": vmem((1, plan.tiles), jnp.int32),
        "col_v": vmem((1, plan.tiles), jnp.int32),
        "count_v": vmem((1, 1), jnp.int32),
        "get_small": dma((5,)),
        "line": vmem((8, LANES), jnp.int32),
        "order_v": vmem((8, LANES), jnp.int32),
        "order": pltpu.SMEM((8, LANES), jnp.int32),
        "lists": vmem((LISTS, LANES), jnp.int32),
        "idx": pltpu.SMEM((LISTS, LANES), jnp.int32),
        "wg": vmem((CORES, nf, width, cols), F32),
        "wg0": vmem((nf, width, cols), BF16),
        "wg_c": vmem((nf, width, cols), BF16),
        "wg1": vmem((plan.xs - 1, nf, rows, cols), BF16),
        "wg_x": vmem((plan.xs - 1, nf, rows, cols), BF16),
        "wg2": vmem((nf, rows, cols), F32),
        "wg2b": vmem((nf, rows, cols), BF16),
        "wg_z": vmem((plan.zs, rows, cols), BF16),
        "wg3": vmem((rows, cols), BF16),
        "wg_y": vmem((nf - 1, rows, cols), BF16),
        "wg4": vmem((rows, cols), F32),
        "wg5": vmem((CORES, plan.xs, rows, cols), F32),
        "bsend": vmem((halo, width, BLK), BF16),
        "brecv": vmem((halo, width, BLK), BF16),
        "bsum": vmem((plan.local + 1, width, BLK), F32),
        "rsum": vmem((halo + 1, width, BLK), F32),
        "get": dma((6,)),
        "halo_s": dma((halo,)), "halo_r": dma((halo,)),
        "w_s": dma((nf - 1,)), "w_r": dma((nf - 1,)),
        "wqx_s": dma((plan.xs - 1,)), "wqx_r": dma((plan.xs - 1,)),
        "wsw": dma((2,)),
        "up_s": dma((ns, nf - 1)), "up_r": dma((ns, nf - 1)),
        "ag_s": dma((ns, nf - 1)), "ag_r": dma((ns, nf - 1)),
        "gr_s": dma((ns, nf - 1)), "gr_r": dma((ns, nf - 1)),
        "back_s": dma((halo,)), "back_r": dma((halo,)),
        "wc": dma((2,)),
        "wx_s": dma((plan.xs - 1,)), "wx_r": dma((plan.xs - 1,)),
        "wz_s": dma((plan.zs - 1,)), "wz_r": dma((plan.zs - 1,)),
        "wy_s": dma((nf - 1,)), "wy_r": dma((nf - 1,)),
        "wl_s": dma((CORES * plan.xs - 1,)), "wl_r": dma((CORES * plan.xs - 1,)),
    }


def local(offsets_of, x_chips, features, weight, tile_row, tile_col, tile_count, send_blocks, tile_values, upstream):
    rows_dev, width = features.shape
    blocks = rows_dev // BLK
    nodes, feats = lax.axis_size("node"), lax.axis_size("feat")
    plan = Plan(blocks, width, tile_row.shape[0], feats, nodes, offsets_of(nodes), x_chips)
    scratch = scratch_of(plan)
    names = list(scratch)
    given = 8

    def body(*refs):
        s = Scratch()
        for name, ref in zip(names, refs[given + 2 :]):
            setattr(s, name, ref)
        kernel(plan, *refs[: given + 2], s)

    anywhere = pl.BlockSpec(memory_space=pltpu.HBM)
    in_vmem = pl.BlockSpec(memory_space=pltpu.VMEM)
    grad_t, weight_sum = pl.pallas_call(
        body,
        out_shape=(
            pltpu.VMEM((width, rows_dev), BF16),
            pltpu.VMEM((width, plan.full), F32),
        ),
        in_specs=[anywhere] * given,
        out_specs=(in_vmem, in_vmem),
        scratch_shapes=[scratch[name] for name in names],
        compiler_params=pltpu.CompilerParams(
            collective_id=0, has_side_effects=True, vmem_limit_bytes=62 * 1024 * 1024
        ),
    )(
        tile_count.reshape(1, 1), send_blocks.reshape(1, nodes), tile_row.reshape(1, -1), tile_col.reshape(1, -1),
        features.T, upstream.T, weight, tile_values,
    )
    return grad_t.T, weight_sum / math.sqrt(rows_dev * nodes)


def build(mesh, offsets_of, x_chips):
    in_specs = (
        P("node", "feat"),
        P("feat", None),
        P("node"),
        P("node"),
        P("node"),
        P("node", None, None),
        P("node", None, None),
        P("node", "feat"),
    )
    out_specs = (P("node", "feat"), P("feat", None))
    return jax.shard_map(
        functools.partial(local, offsets_of, x_chips), mesh=mesh, in_specs=in_specs, out_specs=out_specs, check_vma=False
    )


def solution(mesh):
    return build(mesh, halo_offsets, X_CHIPS)
```

```python
import functools
import math

import jax
import jax.numpy as jnp
from jax import lax
from jax.experimental import pallas as pl
from jax.experimental.pallas import tpu as pltpu
from jax.sharding import PartitionSpec as P

MESH = pl.DeviceIdType.MESH
F32 = jnp.float32
BF16 = jnp.bfloat16
BLK = 128
CORES = 2
X_CHIPS = 4


def halo_offsets(node_count):
    near = [step for d in range(1, 8) for step in (d, -d)]
    return near + [8, 32]


class Plan:
    def __init__(self, blocks, width, tiles, feats, nodes, offsets, x_chips):
        self.blocks, self.width, self.tiles = blocks, width, tiles
        self.feats, self.nodes, self.offsets = feats, nodes, offsets
        self.halo = len(offsets)
        self.local = tiles - self.halo
        self.full = width * feats
        self.stages = blocks // (2 * feats)
        self.xs = x_chips
        self.zs = nodes // (CORES * x_chips)


LANES = 128
BITS = 7
MASK = (1 << BITS) - 1
(FL_T, FL_C, FL_K, FL_END, FH_T, FH_S, FH_K, FH_END, BH_T, BH_R, BL_T, BL_R, BL_K, BL_END, R_S, R_K, R_END) = range(17)
LISTS = 24
HELD = 5


def iota(dim, rows=LANES):
    return lax.broadcasted_iota(jnp.int32, (rows, LANES), dim)


def as_columns(vector):
    return jnp.broadcast_to(vector, (LANES, LANES)).T


def count(where):
    return jnp.sum(jnp.where(where, 1, 0), axis=0, keepdims=True)


def pick(one_hot, columns):
    return jnp.sum(jnp.where(one_hot, columns, 0), axis=0, keepdims=True)


def in_order(group, first, second):
    lane, sub = iota(1), iota(0)
    down = as_columns(group)
    smaller = count(down < group)
    rank = smaller + count(jnp.logical_and(down == group, sub < lane))
    follows = jnp.where(rank > smaller, 1, 0)
    packed = as_columns(rank + (first << BITS) + (second << (2 * BITS)) + (follows << (3 * BITS)))
    got = pick((packed & MASK) == lane, packed >> BITS)
    end = jnp.where(count(down == lane) > 0, count(down <= lane), 0)
    return got & MASK, (got >> BITS) & MASK, got >> (2 * BITS), end


def write_order(plan, node, live, row_ref, col_ref, send_ref, line, first):
    n = plan.nodes
    lane = iota(1, 1)
    line[...] = jnp.zeros_like(line)
    line[0:1, 0 : plan.tiles] = row_ref[...]
    line[1:2, 0 : plan.tiles] = col_ref[...]
    line[2:3, 0:n] = send_ref[...]
    row, col = line[0:1, :], line[1:2, :]
    alive = lane < live
    reads = jnp.full((1, LANES), -1, jnp.int32)
    for i, d in enumerate(plan.offsets):
        reads = jnp.where(lane == i, plan.blocks + lax.rem(node + d + n, n), reads)
    packed = as_columns(jnp.where(alive, col + (row << BITS), 0))
    got = pick((packed & MASK) == reads, (packed >> BITS) + (iota(0) << BITS))
    bh_t, bh_r = got >> BITS, got & MASK
    rows_used = as_columns(jnp.where(lane < plan.halo, bh_r, plan.blocks))
    group = jnp.where(lane < plan.blocks, jnp.where(count(rows_used == lane) > 0, 0, 1), 2)
    down = as_columns(group)
    place = count(down < group) + count(jnp.logical_and(down == group, iota(0) < iota(1)))
    place_down = as_columns(place)
    order = pick(place_down == lane, iota(0))
    first[...] = jnp.zeros_like(first)
    first[0:1, :] = order
    return bh_t, bh_r, place_down


def write_lists(plan, node, live, order, line, lists):
    n = plan.nodes
    lane = iota(1, 1)
    bh_t, bh_r, place_down = order
    row, col, sends = line[0:1, :], line[1:2, :], line[2:3, :]
    local = jnp.logical_and(lane < live, col < plan.blocks)
    row_in, col_in = jnp.where(local, row, plan.blocks), jnp.where(local, col, plan.blocks)
    fl_t, fl_c, fl_k, fl_end = in_order(row_in, lane, col_in)
    bl_t, bl_r, bl_k, bl_end = in_order(col_in, lane, pick(iota(0) == row_in, place_down))
    serves = jnp.full((1, LANES), -1, jnp.int32)
    for i, d in enumerate(plan.offsets):
        serves = jnp.where(lane == i, lax.rem(node - d + n, n), serves)
    target = pick(iota(0) == serves, as_columns(sends))
    used = lane < plan.halo
    fh_t, fh_s, fh_k, fh_end = in_order(jnp.where(used, bh_r, plan.blocks), bh_t, lane)
    r_s, _, r_k, r_end = in_order(jnp.where(used, target, plan.blocks), lane, lane)
    bh_p = pick(iota(0) == bh_r, place_down)
    rows = [fl_t, fl_c, fl_k, fl_end, fh_t, fh_s, fh_k, fh_end, bh_t, bh_p, bl_t, bl_r, bl_k, bl_end, r_s, r_k, r_end]
    lists[...] = jnp.zeros_like(lists)
    for i, vector in enumerate(rows):
        lists[i : i + 1, :] = vector


def kernel(plan, count_hbm, send_hbm, row_hbm, col_hbm, feats_hbm, up_hbm, w_hbm, tiles_hbm, out_ref, wout_ref, s):
    nf, nn, width = plan.feats, plan.nodes, plan.width
    zs, xs = plan.zs, plan.xs
    rows, cols = width // xs, plan.full // CORES
    pair = 2 * BLK
    node, f = lax.axis_index("node"), lax.axis_index("feat")
    c = lax.rem(node, CORES)
    x = lax.rem(node // CORES, xs)
    z = node // (CORES * xs)
    idx = s.idx

    def node_of(z_at, x_at, c_at):
        return (z_at * xs + x_at) * CORES + c_at

    def remote(src, dst, send_sem, recv_sem, to):
        return pltpu.make_async_remote_copy(
            src_ref=src, dst_ref=dst, send_sem=send_sem, recv_sem=recv_sem, device_id=to, device_id_type=MESH
        )

    near = sorted({d % nn for d in plan.offsets} | {-d % nn for d in plan.offsets})
    z_far_first = sorted(range(1, zs), key=lambda d: -min(d, zs - d))
    x_far_first = sorted(range(1, xs), key=lambda d: -min(d, xs - d))
    plane = [(dx, dc) for dx in x_far_first for dc in range(CORES)] + [(0, 1)]
    partners = [(node_of(lax.rem(z + d, zs), x, c), f) for d in z_far_first if d * xs * CORES not in near]
    partners += [(lax.rem(node + d, nn), f) for d in near]
    partners += [(node_of(z, lax.rem(x + dx, xs), lax.rem(c + dc, CORES)), f) for dx, dc in plane]
    partners += [(node, lax.rem(f + d, nf)) for d in range(1, nf)]
    barrier = pltpu.get_barrier_semaphore()
    for to in partners:
        pl.semaphore_signal(barrier, inc=1, device_id=to, device_id_type=MESH)

    get_feats = pltpu.make_async_copy(feats_hbm, s.feats, s.get.at[0])
    get_w = pltpu.make_async_copy(
        w_hbm.at[pl.ds(x * rows, rows), pl.ds(pl.multiple_of(c * cols, cols), cols)], s.wq.at[c, x, f], s.get.at[1]
    )
    get_tiles = pltpu.make_async_copy(tiles_hbm, s.tiles, s.get.at[2])
    get_up = pltpu.make_async_copy(up_hbm, s.up, s.get.at[3])
    get_send = pltpu.make_async_copy(send_hbm, s.send_sm, s.get_small.at[0])
    get_lines = [
        pltpu.make_async_copy(src, dst, s.get_small.at[1 + i])
        for i, (src, dst) in enumerate(
            [(send_hbm, s.send_v), (row_hbm, s.row_v), (col_hbm, s.col_v), (count_hbm, s.count_v)]
        )
    ]
    for copy in get_lines + [get_up, get_w, get_send, get_feats, get_tiles]:
        copy.start()

    for copy in get_lines:
        copy.wait()
    live = s.count_v[...]
    order = write_order(plan, node, live, s.row_v, s.col_v, s.send_v, s.line, s.order_v)
    put_order = pltpu.make_async_copy(s.order_v, s.order, s.get.at[4])
    put_order.start()

    get_up.wait()
    for b in range(plan.blocks):
        s.uptable[b] = s.up[:, b * BLK : (b + 1) * BLK]
    get_w.wait()
    pl.semaphore_wait(barrier, len(partners))

    far_first = sorted(range(1, nf), key=lambda d: -min(d, nf - d))
    w_copies = [
        remote(s.wq.at[c, x, f], s.wq.at[c, x, f], s.w_s.at[d - 1], s.w_r.at[d - 1], (node, lax.rem(f + d, nf)))
        for d in far_first
    ]
    for copy in w_copies:
        copy.start()

    put_order.wait()
    up_copies = []

    def send_up(k):
        stage_copies = []
        for d in far_first + [0]:
            j = lax.rem(f + d, nf)
            p = k * nf + j
            into = s.upk.at[p] if d else s.ur.at[k, f]
            into[:, 0:BLK] = s.uptable[s.order[0, 2 * p]]
            into[:, BLK:pair] = s.uptable[s.order[0, 2 * p + 1]]
            if d:
                copy = remote(s.upk.at[p], s.ur.at[k, f], s.up_s.at[k, d - 1], s.up_r.at[k, d - 1], (node, j))
                copy.start()
                stage_copies.append(copy)
        up_copies.append(stage_copies)

    send_up(0)
    get_feats.wait()
    get_send.wait()
    for b in range(plan.blocks):
        s.table[b] = s.feats[:, b * BLK : (b + 1) * BLK]
    s.table[plan.blocks] = jnp.zeros((width, BLK), BF16)
    halo_copies = []
    for i, d in enumerate(plan.offsets):
        to = lax.rem(node - d + nn, nn)
        s.hsend[i] = s.table[s.send_sm[0, to]]
        copy = remote(s.hsend.at[i], s.hrecv.at[i], s.halo_s.at[i], s.halo_r.at[i], (to, f))
        copy.start()
        halo_copies.append(copy)

    for k in range(1, plan.stages):
        send_up(k)

    write_lists(plan, node, live, order, s.line, s.lists)
    put_lists = pltpu.make_async_copy(s.lists, s.idx, s.get.at[5])
    put_lists.start()
    zero = jnp.zeros((width, BLK), F32)
    for ref in (s.fsum, s.hsum, s.bsum, s.rsum):
        ref[0] = zero
    s.grad[plan.blocks] = jnp.zeros((width, BLK), BF16)

    for copy in w_copies:
        copy.wait()
    wx_copies = []
    for d in x_far_first:
        to = (node_of(z, lax.rem(x + d, xs), c), f)
        wx_copies.append(remote(s.wq.at[c, x], s.wq.at[c, x], s.wqx_s.at[d - 1], s.wqx_r.at[d - 1], to))
    for copy in wx_copies:
        copy.start()

    put_lists.wait()
    get_tiles.wait()

    def forward_local(i, total):
        keep = idx[FL_K, i].astype(F32)
        term = lax.dot_general(
            s.table[idx[FL_C, i]], s.tiles[idx[FL_T, i]], (((1,), (1,)), ((), ())), preferred_element_type=F32
        )
        total = total * keep + term
        s.fsum[i + 1] = total
        return total

    lax.fori_loop(0, plan.local, forward_local, zero, unroll=16)

    for copy in halo_copies:
        copy.wait()

    def forward_halo(i, total):
        keep = idx[FH_K, i].astype(F32)
        term = lax.dot_general(
            s.hrecv[idx[FH_S, i]], s.tiles[idx[FH_T, i]], (((1,), (1,)), ((), ())), preferred_element_type=F32
        )
        total = total * keep + term
        s.hsum[i + 1] = total
        return total

    lax.fori_loop(0, plan.halo, forward_halo, zero, unroll=plan.halo)

    def summed(at):
        b = s.order[0, at]
        return (s.fsum[idx[FL_END, b]] + s.hsum[idx[FH_END, b]]).astype(BF16)

    agg_copies = []
    for k in range(plan.stages):
        stage_copies = []
        for d in far_first + [0]:
            j = lax.rem(f + d, nf)
            p = k * nf + j
            into = s.apk.at[p] if d else s.ar.at[k, f]
            into[:, 0:BLK] = summed(2 * p)
            into[:, BLK:pair] = summed(2 * p + 1)
            if d:
                copy = remote(s.apk.at[p], s.ar.at[k, f], s.ag_s.at[k, d - 1], s.ag_r.at[k, d - 1], (node, j))
                copy.start()
                stage_copies.append(copy)
        agg_copies.append(stage_copies)

    for copy in wx_copies:
        copy.wait()
    other = (node_of(z, x, 1 - c), f)
    w_swap = remote(s.wq.at[c], s.wq.at[c], s.wsw.at[0], s.wsw.at[1], other)
    w_swap.start()
    w_swap.wait()
    for j in range(nf):
        for at in range(xs):
            for h in range(CORES):
                s.wfull[pl.ds(j * width + at * rows, rows), pl.ds(h * cols, cols)] = s.wq[h, at, j]
    s.wt[...] = s.wfull[...].T

    grad_copies = [[] for _ in range(plan.stages)]

    def send_grad(k, distances):
        for d in distances:
            j = lax.rem(f + d, nf)
            into = s.first.at[pl.ds(2 * f, 2)] if k == 0 else s.grad.at[pl.ds(2 * (k * nf + f), 2)]
            copy = remote(s.gsend.at[k, j], into, s.gr_s.at[k, d - 1], s.gr_r.at[k, d - 1], (node, j))
            copy.start()
            grad_copies[k].append(copy)

    for k in range(plan.stages):
        for copy in up_copies[k] + agg_copies[k]:
            copy.wait()
        if k:
            send_grad(k - 1, far_first)
        agg = s.ar[k].reshape(plan.full, pair)
        pre = jnp.dot(s.wt[...], agg, preferred_element_type=F32)
        sig = jax.nn.sigmoid(pre)
        upstream = s.ur[k].reshape(plan.full, pair).astype(F32)
        s.gp[...] = (upstream * sig * (1.0 + pre * (1.0 - sig))).astype(BF16)

        def weight_part(h):
            columns = s.gp[pl.ds(pl.multiple_of(h * cols, cols), cols)]
            wg = lax.dot_general(agg, columns, (((1,), (1,)), ((), ())), preferred_element_type=F32)
            return wg.reshape(nf, width, cols) + (s.wg[h] if k else 0.0)

        last = k == plan.stages - 1
        if last:
            s.wg0[...] = weight_part(1 - c).astype(BF16)
            wg_core = remote(s.wg0, s.wg_c, s.wc.at[0], s.wc.at[1], other)
            wg_core.start()
        grad = jnp.dot(s.wfull[...], s.gp[...], preferred_element_type=F32).astype(BF16)
        for j in range(nf):
            for h in range(2):
                s.gsend[k, j, h] = grad[j * width : (j + 1) * width, h * BLK : (h + 1) * BLK]
        if last:
            send_grad(k, far_first[HELD:])
        into = s.first.at[pl.ds(2 * f, 2)] if k == 0 else s.grad.at[pl.ds(2 * (k * nf + f), 2)]
        into[...] = s.gsend[k, f]
        if last:
            s.wg[c] = weight_part(c)
        else:
            for h in range(CORES):
                s.wg[h] = weight_part(h)

    wg_core.wait()
    x_copies = []
    for d in x_far_first + [0]:
        to_x = lax.rem(x + d, xs)
        at = pl.ds(pl.multiple_of(to_x * rows, rows), rows)
        part = s.wg[c, :, at, :] + s.wg_c[:, at, :].astype(F32)
        if d:
            s.wg1[d - 1] = part.astype(BF16)
            to = (node_of(z, to_x, c), f)
            copy = remote(s.wg1.at[d - 1], s.wg_x.at[d - 1], s.wx_s.at[d - 1], s.wx_r.at[d - 1], to)
            copy.start()
            x_copies.append(copy)
        else:
            s.wg2[...] = part
    for copy in x_copies:
        copy.wait()
    s.wg2[...] = sum([s.wg_x[d].astype(F32) for d in range(xs - 1)], s.wg2[...])
    s.wg2b[...] = s.wg2[...].astype(BF16)
    y_copies = []
    for d in far_first:
        j = lax.rem(f + d, nf)
        copy = remote(s.wg2b.at[j], s.wg_y.at[d - 1], s.wy_s.at[d - 1], s.wy_r.at[d - 1], (node, j))
        copy.start()
        y_copies.append(copy)
    send_grad(plan.stages - 1, far_first[:HELD])
    for copy in grad_copies[0]:
        copy.wait()
    back_copies = []
    for i, d in enumerate(plan.offsets):
        term = jnp.dot(s.first[idx[BH_R, i]], s.tiles[idx[BH_T, i]], preferred_element_type=F32)
        s.bsend[i] = term.astype(BF16)
        copy = remote(
            s.bsend.at[i], s.brecv.at[i], s.back_s.at[i], s.back_r.at[i], (lax.rem(node + d + nn, nn), f)
        )
        copy.start()
        back_copies.append(copy)
    s.grad[pl.ds(0, 2 * nf)] = s.first[...]

    for copy in y_copies:
        copy.wait()
    s.wg3[...] = sum([s.wg_y[d].astype(F32) for d in range(nf - 1)], s.wg2[f]).astype(BF16)
    s.wg_z[z] = s.wg3[...]
    z_copies = []
    for d in z_far_first:
        to = (node_of(lax.rem(z + d, zs), x, c), f)
        copy = remote(s.wg3, s.wg_z.at[z], s.wz_s.at[d - 1], s.wz_r.at[d - 1], to)
        copy.start()
        z_copies.append(copy)

    for copy in z_copies:
        copy.wait()
    s.wg4[...] = sum([s.wg_z[at].astype(F32) for at in range(1, zs)], s.wg_z[0].astype(F32))
    s.wg5[c, x] = s.wg4[...]
    last_copies = []
    for i, (dx, dc) in enumerate(plane):
        to = (node_of(z, lax.rem(x + dx, xs), lax.rem(c + dc, CORES)), f)
        copy = remote(s.wg4, s.wg5.at[c, x], s.wl_s.at[i], s.wl_r.at[i], to)
        copy.start()
        last_copies.append(copy)

    for copy in sum(grad_copies[1:], []):
        copy.wait()

    def backward_local(i, total):
        keep = idx[BL_K, i].astype(F32)
        term = jnp.dot(s.grad[idx[BL_R, i]], s.tiles[idx[BL_T, i]], preferred_element_type=F32)
        total = total * keep + term
        s.bsum[i + 1] = total
        return total

    lax.fori_loop(0, plan.local, backward_local, zero, unroll=16)

    for copy in back_copies:
        copy.wait()

    def returned(i, total):
        keep = idx[R_K, i].astype(F32)
        total = total * keep + s.brecv[idx[R_S, i]].astype(F32)
        s.rsum[i + 1] = total
        return total

    lax.fori_loop(0, plan.halo, returned, zero, unroll=plan.halo)

    for b in range(plan.blocks):
        out_ref[:, b * BLK : (b + 1) * BLK] = (s.bsum[idx[BL_END, b]] + s.rsum[idx[R_END, b]]).astype(BF16)

    for copy in last_copies:
        copy.wait()
    for h in range(CORES):
        for at in range(xs):
            wout_ref[pl.ds(at * rows, rows), pl.ds(h * cols, cols)] = s.wg5[h, at]


class Scratch:
    pass


def scratch_of(plan):
    nf, ns, halo, blocks, width = plan.feats, plan.stages, plan.halo, plan.blocks, plan.width
    cols, rows = plan.full // CORES, width // plan.xs
    dma = pltpu.SemaphoreType.DMA
    vmem = pltpu.VMEM
    return {
        "feats": vmem((width, blocks * BLK), BF16),
        "table": vmem((blocks + 1, width, BLK), BF16),
        "up": vmem((width, blocks * BLK), BF16),
        "uptable": vmem((blocks, width, BLK), BF16),
        "upk": vmem((blocks // 2, width, 2 * BLK), BF16),
        "ur": vmem((ns, nf, width, 2 * BLK), BF16),
        "wq": vmem((CORES, plan.xs, nf, rows, cols), BF16),
        "wfull": vmem((plan.full, plan.full), BF16),
        "wt": vmem((plan.full, plan.full), BF16),
        "tiles": vmem((plan.tiles, BLK, BLK), BF16),
        "hsend": vmem((halo, width, BLK), BF16),
        "hrecv": vmem((halo, width, BLK), BF16),
        "fsum": vmem((plan.local + 1, width, BLK), F32),
        "hsum": vmem((halo + 1, width, BLK), F32),
        "apk": vmem((blocks // 2, width, 2 * BLK), BF16),
        "ar": vmem((ns, nf, width, 2 * BLK), BF16),
        "gp": vmem((plan.full, 2 * BLK), BF16),
        "gsend": vmem((ns, nf, 2, width, BLK), BF16),
        "first": vmem((2 * nf, width, BLK), BF16),
        "grad": vmem((blocks + 1, width, BLK), BF16),
        "send_sm": pltpu.SMEM((1, plan.nodes), jnp.int32),
        "send_v": vmem((1, plan.nodes), jnp.int32),
        "row_v": vmem((1, plan.tiles), jnp.int32),
        "col_v": vmem((1, plan.tiles), jnp.int32),
        "count_v": vmem((1, 1), jnp.int32),
        "get_small": dma((5,)),
        "line": vmem((8, LANES), jnp.int32),
        "order_v": vmem((8, LANES), jnp.int32),
        "order": pltpu.SMEM((8, LANES), jnp.int32),
        "lists": vmem((LISTS, LANES), jnp.int32),
        "idx": pltpu.SMEM((LISTS, LANES), jnp.int32),
        "wg": vmem((CORES, nf, width, cols), F32),
        "wg0": vmem((nf, width, cols), BF16),
        "wg_c": vmem((nf, width, cols), BF16),
        "wg1": vmem((plan.xs - 1, nf, rows, cols), BF16),
        "wg_x": vmem((plan.xs - 1, nf, rows, cols), BF16),
        "wg2": vmem((nf, rows, cols), F32),
        "wg2b": vmem((nf, rows, cols), BF16),
        "wg_z": vmem((plan.zs, rows, cols), BF16),
        "wg3": vmem((rows, cols), BF16),
        "wg_y": vmem((nf - 1, rows, cols), BF16),
        "wg4": vmem((rows, cols), F32),
        "wg5": vmem((CORES, plan.xs, rows, cols), F32),
        "bsend": vmem((halo, width, BLK), BF16),
        "brecv": vmem((halo, width, BLK), BF16),
        "bsum": vmem((plan.local + 1, width, BLK), F32),
        "rsum": vmem((halo + 1, width, BLK), F32),
        "get": dma((6,)),
        "halo_s": dma((halo,)), "halo_r": dma((halo,)),
        "w_s": dma((nf - 1,)), "w_r": dma((nf - 1,)),
        "wqx_s": dma((plan.xs - 1,)), "wqx_r": dma((plan.xs - 1,)),
        "wsw": dma((2,)),
        "up_s": dma((ns, nf - 1)), "up_r": dma((ns, nf - 1)),
        "ag_s": dma((ns, nf - 1)), "ag_r": dma((ns, nf - 1)),
        "gr_s": dma((ns, nf - 1)), "gr_r": dma((ns, nf - 1)),
        "back_s": dma((halo,)), "back_r": dma((halo,)),
        "wc": dma((2,)),
        "wx_s": dma((plan.xs - 1,)), "wx_r": dma((plan.xs - 1,)),
        "wz_s": dma((plan.zs - 1,)), "wz_r": dma((plan.zs - 1,)),
        "wy_s": dma((nf - 1,)), "wy_r": dma((nf - 1,)),
        "wl_s": dma((CORES * plan.xs - 1,)), "wl_r": dma((CORES * plan.xs - 1,)),
    }


def local(offsets_of, x_chips, features, weight, tile_row, tile_col, tile_count, send_blocks, tile_values, upstream):
    rows_dev, width = features.shape
    blocks = rows_dev // BLK
    nodes, feats = lax.axis_size("node"), lax.axis_size("feat")
    plan = Plan(blocks, width, tile_row.shape[0], feats, nodes, offsets_of(nodes), x_chips)
    scratch = scratch_of(plan)
    names = list(scratch)
    given = 8

    def body(*refs):
        s = Scratch()
        for name, ref in zip(names, refs[given + 2 :]):
            setattr(s, name, ref)
        kernel(plan, *refs[: given + 2], s)

    anywhere = pl.BlockSpec(memory_space=pltpu.HBM)
    in_vmem = pl.BlockSpec(memory_space=pltpu.VMEM)
    grad_t, weight_sum = pl.pallas_call(
        body,
        out_shape=(
            pltpu.VMEM((width, rows_dev), BF16),
            pltpu.VMEM((width, plan.full), F32),
        ),
        in_specs=[anywhere] * given,
        out_specs=(in_vmem, in_vmem),
        scratch_shapes=[scratch[name] for name in names],
        compiler_params=pltpu.CompilerParams(
            collective_id=0, has_side_effects=True, vmem_limit_bytes=62 * 1024 * 1024
        ),
    )(
        tile_count.reshape(1, 1), send_blocks.reshape(1, nodes), tile_row.reshape(1, -1), tile_col.reshape(1, -1),
        features.T, upstream.T, weight, tile_values,
    )
    return grad_t.T, weight_sum / math.sqrt(rows_dev * nodes)


def build(mesh, offsets_of, x_chips):
    in_specs = (
        P("node", "feat"),
        P("feat", None),
        P("node"),
        P("node"),
        P("node"),
        P("node", None, None),
        P("node", None, None),
        P("node", "feat"),
    )
    out_specs = (P("node", "feat"), P("feat", None))
    return jax.shard_map(
        functools.partial(local, offsets_of, x_chips), mesh=mesh, in_specs=in_specs, out_specs=out_specs, check_vma=False
    )


def solution(mesh):
    return build(mesh, halo_offsets, X_CHIPS)
```

```python
import functools
import math

import jax
import jax.numpy as jnp
from jax import lax
from jax.experimental import pallas as pl
from jax.experimental.pallas import tpu as pltpu
from jax.sharding import PartitionSpec as P

MESH = pl.DeviceIdType.MESH
F32 = jnp.float32
BF16 = jnp.bfloat16
BLK = 128
CORES = 2
X_CHIPS = 4


def halo_offsets(node_count):
    near = [step for d in range(1, 8) for step in (d, -d)]
    return near + [8, 32]


class Plan:
    def __init__(self, blocks, width, tiles, feats, nodes, offsets, x_chips):
        self.blocks, self.width, self.tiles = blocks, width, tiles
        self.feats, self.nodes, self.offsets = feats, nodes, offsets
        self.halo = len(offsets)
        self.local = tiles - self.halo
        self.full = width * feats
        self.stages = blocks // (2 * feats)
        self.xs = x_chips
        self.zs = nodes // (CORES * x_chips)


LANES = 128
BITS = 7
MASK = (1 << BITS) - 1
(FL_T, FL_C, FL_K, FL_END, FH_T, FH_S, FH_K, FH_END, BH_T, BH_R, BL_T, BL_R, BL_K, BL_END, R_S, R_K, R_END) = range(17)
LISTS = 24
HELD = 7


def iota(dim, rows=LANES):
    return lax.broadcasted_iota(jnp.int32, (rows, LANES), dim)


def as_columns(vector):
    return jnp.broadcast_to(vector, (LANES, LANES)).T


def count(where):
    return jnp.sum(jnp.where(where, 1, 0), axis=0, keepdims=True)


def pick(one_hot, columns):
    return jnp.sum(jnp.where(one_hot, columns, 0), axis=0, keepdims=True)


def in_order(group, first, second):
    lane, sub = iota(1), iota(0)
    down = as_columns(group)
    smaller = count(down < group)
    rank = smaller + count(jnp.logical_and(down == group, sub < lane))
    follows = jnp.where(rank > smaller, 1, 0)
    packed = as_columns(rank + (first << BITS) + (second << (2 * BITS)) + (follows << (3 * BITS)))
    got = pick((packed & MASK) == lane, packed >> BITS)
    end = jnp.where(count(down == lane) > 0, count(down <= lane), 0)
    return got & MASK, (got >> BITS) & MASK, got >> (2 * BITS), end


def write_order(plan, node, live, row_ref, col_ref, send_ref, line, first):
    n = plan.nodes
    lane = iota(1, 1)
    line[...] = jnp.zeros_like(line)
    line[0:1, 0 : plan.tiles] = row_ref[...]
    line[1:2, 0 : plan.tiles] = col_ref[...]
    line[2:3, 0:n] = send_ref[...]
    row, col = line[0:1, :], line[1:2, :]
    alive = lane < live
    reads = jnp.full((1, LANES), -1, jnp.int32)
    for i, d in enumerate(plan.offsets):
        reads = jnp.where(lane == i, plan.blocks + lax.rem(node + d + n, n), reads)
    packed = as_columns(jnp.where(alive, col + (row << BITS), 0))
    got = pick((packed & MASK) == reads, (packed >> BITS) + (iota(0) << BITS))
    bh_t, bh_r = got >> BITS, got & MASK
    rows_used = as_columns(jnp.where(lane < plan.halo, bh_r, plan.blocks))
    group = jnp.where(lane < plan.blocks, jnp.where(count(rows_used == lane) > 0, 0, 1), 2)
    down = as_columns(group)
    place = count(down < group) + count(jnp.logical_and(down == group, iota(0) < iota(1)))
    place_down = as_columns(place)
    order = pick(place_down == lane, iota(0))
    first[...] = jnp.zeros_like(first)
    first[0:1, :] = order
    return bh_t, bh_r, place_down


def write_lists(plan, node, live, order, line, lists):
    n = plan.nodes
    lane = iota(1, 1)
    bh_t, bh_r, place_down = order
    row, col, sends = line[0:1, :], line[1:2, :], line[2:3, :]
    local = jnp.logical_and(lane < live, col < plan.blocks)
    row_in, col_in = jnp.where(local, row, plan.blocks), jnp.where(local, col, plan.blocks)
    fl_t, fl_c, fl_k, fl_end = in_order(row_in, lane, col_in)
    bl_t, bl_r, bl_k, bl_end = in_order(col_in, lane, pick(iota(0) == row_in, place_down))
    serves = jnp.full((1, LANES), -1, jnp.int32)
    for i, d in enumerate(plan.offsets):
        serves = jnp.where(lane == i, lax.rem(node - d + n, n), serves)
    target = pick(iota(0) == serves, as_columns(sends))
    used = lane < plan.halo
    fh_t, fh_s, fh_k, fh_end = in_order(jnp.where(used, bh_r, plan.blocks), bh_t, lane)
    r_s, _, r_k, r_end = in_order(jnp.where(used, target, plan.blocks), lane, lane)
    bh_p = pick(iota(0) == bh_r, place_down)
    rows = [fl_t, fl_c, fl_k, fl_end, fh_t, fh_s, fh_k, fh_end, bh_t, bh_p, bl_t, bl_r, bl_k, bl_end, r_s, r_k, r_end]
    lists[...] = jnp.zeros_like(lists)
    for i, vector in enumerate(rows):
        lists[i : i + 1, :] = vector


def kernel(plan, count_hbm, send_hbm, row_hbm, col_hbm, feats_hbm, up_hbm, w_hbm, tiles_hbm, out_ref, wout_ref, s):
    nf, nn, width = plan.feats, plan.nodes, plan.width
    zs, xs = plan.zs, plan.xs
    rows, cols = width // xs, plan.full // CORES
    pair = 2 * BLK
    node, f = lax.axis_index("node"), lax.axis_index("feat")
    c = lax.rem(node, CORES)
    x = lax.rem(node // CORES, xs)
    z = node // (CORES * xs)
    idx = s.idx

    def node_of(z_at, x_at, c_at):
        return (z_at * xs + x_at) * CORES + c_at

    def remote(src, dst, send_sem, recv_sem, to):
        return pltpu.make_async_remote_copy(
            src_ref=src, dst_ref=dst, send_sem=send_sem, recv_sem=recv_sem, device_id=to, device_id_type=MESH
        )

    near = sorted({d % nn for d in plan.offsets} | {-d % nn for d in plan.offsets})
    z_far_first = sorted(range(1, zs), key=lambda d: -min(d, zs - d))
    x_far_first = sorted(range(1, xs), key=lambda d: -min(d, xs - d))
    plane = [(dx, dc) for dx in x_far_first for dc in range(CORES)] + [(0, 1)]
    partners = [(node_of(lax.rem(z + d, zs), x, c), f) for d in z_far_first if d * xs * CORES not in near]
    partners += [(lax.rem(node + d, nn), f) for d in near]
    partners += [(node_of(z, lax.rem(x + dx, xs), lax.rem(c + dc, CORES)), f) for dx, dc in plane]
    partners += [(node, lax.rem(f + d, nf)) for d in range(1, nf)]
    barrier = pltpu.get_barrier_semaphore()
    for to in partners:
        pl.semaphore_signal(barrier, inc=1, device_id=to, device_id_type=MESH)

    get_feats = pltpu.make_async_copy(feats_hbm, s.feats, s.get.at[0])
    get_w = pltpu.make_async_copy(
        w_hbm.at[pl.ds(x * rows, rows), pl.ds(pl.multiple_of(c * cols, cols), cols)], s.wq.at[c, x, f], s.get.at[1]
    )
    get_tiles = pltpu.make_async_copy(tiles_hbm, s.tiles, s.get.at[2])
    get_up = pltpu.make_async_copy(up_hbm, s.up, s.get.at[3])
    get_send = pltpu.make_async_copy(send_hbm, s.send_sm, s.get_small.at[0])
    get_lines = [
        pltpu.make_async_copy(src, dst, s.get_small.at[1 + i])
        for i, (src, dst) in enumerate(
            [(send_hbm, s.send_v), (row_hbm, s.row_v), (col_hbm, s.col_v), (count_hbm, s.count_v)]
        )
    ]
    for copy in get_lines + [get_up, get_w, get_send, get_feats, get_tiles]:
        copy.start()

    for copy in get_lines:
        copy.wait()
    live = s.count_v[...]
    order = write_order(plan, node, live, s.row_v, s.col_v, s.send_v, s.line, s.order_v)
    put_order = pltpu.make_async_copy(s.order_v, s.order, s.get.at[4])
    put_order.start()

    get_up.wait()
    for b in range(plan.blocks):
        s.uptable[b] = s.up[:, b * BLK : (b + 1) * BLK]
    get_w.wait()
    pl.semaphore_wait(barrier, len(partners))

    far_first = sorted(range(1, nf), key=lambda d: -min(d, nf - d))
    w_copies = [
        remote(s.wq.at[c, x, f], s.wq.at[c, x, f], s.w_s.at[d - 1], s.w_r.at[d - 1], (node, lax.rem(f + d, nf)))
        for d in far_first
    ]
    for copy in w_copies:
        copy.start()

    put_order.wait()
    up_copies = []

    def send_up(k):
        stage_copies = []
        for d in far_first + [0]:
            j = lax.rem(f + d, nf)
            p = k * nf + j
            into = s.upk.at[p] if d else s.ur.at[k, f]
            into[:, 0:BLK] = s.uptable[s.order[0, 2 * p]]
            into[:, BLK:pair] = s.uptable[s.order[0, 2 * p + 1]]
            if d:
                copy = remote(s.upk.at[p], s.ur.at[k, f], s.up_s.at[k, d - 1], s.up_r.at[k, d - 1], (node, j))
                copy.start()
                stage_copies.append(copy)
        up_copies.append(stage_copies)

    send_up(0)
    get_feats.wait()
    get_send.wait()
    for b in range(plan.blocks):
        s.table[b] = s.feats[:, b * BLK : (b + 1) * BLK]
    s.table[plan.blocks] = jnp.zeros((width, BLK), BF16)
    halo_copies = []
    for i, d in enumerate(plan.offsets):
        to = lax.rem(node - d + nn, nn)
        s.hsend[i] = s.table[s.send_sm[0, to]]
        copy = remote(s.hsend.at[i], s.hrecv.at[i], s.halo_s.at[i], s.halo_r.at[i], (to, f))
        copy.start()
        halo_copies.append(copy)

    for k in range(1, plan.stages):
        send_up(k)

    write_lists(plan, node, live, order, s.line, s.lists)
    put_lists = pltpu.make_async_copy(s.lists, s.idx, s.get.at[5])
    put_lists.start()
    zero = jnp.zeros((width, BLK), F32)
    for ref in (s.fsum, s.hsum, s.bsum, s.rsum):
        ref[0] = zero
    s.grad[plan.blocks] = jnp.zeros((width, BLK), BF16)

    for copy in w_copies:
        copy.wait()
    wx_copies = []
    for d in x_far_first:
        to = (node_of(z, lax.rem(x + d, xs), c), f)
        wx_copies.append(remote(s.wq.at[c, x], s.wq.at[c, x], s.wqx_s.at[d - 1], s.wqx_r.at[d - 1], to))
    for copy in wx_copies:
        copy.start()

    put_lists.wait()
    get_tiles.wait()

    def forward_local(i, total):
        keep = idx[FL_K, i].astype(F32)
        term = lax.dot_general(
            s.table[idx[FL_C, i]], s.tiles[idx[FL_T, i]], (((1,), (1,)), ((), ())), preferred_element_type=F32
        )
        total = total * keep + term
        s.fsum[i + 1] = total
        return total

    lax.fori_loop(0, plan.local, forward_local, zero, unroll=16)

    for copy in halo_copies:
        copy.wait()

    def forward_halo(i, total):
        keep = idx[FH_K, i].astype(F32)
        term = lax.dot_general(
            s.hrecv[idx[FH_S, i]], s.tiles[idx[FH_T, i]], (((1,), (1,)), ((), ())), preferred_element_type=F32
        )
        total = total * keep + term
        s.hsum[i + 1] = total
        return total

    lax.fori_loop(0, plan.halo, forward_halo, zero, unroll=plan.halo)

    def summed(at):
        b = s.order[0, at]
        return (s.fsum[idx[FL_END, b]] + s.hsum[idx[FH_END, b]]).astype(BF16)

    agg_copies = []
    for k in range(plan.stages):
        stage_copies = []
        for d in far_first + [0]:
            j = lax.rem(f + d, nf)
            p = k * nf + j
            into = s.apk.at[p] if d else s.ar.at[k, f]
            into[:, 0:BLK] = summed(2 * p)
            into[:, BLK:pair] = summed(2 * p + 1)
            if d:
                copy = remote(s.apk.at[p], s.ar.at[k, f], s.ag_s.at[k, d - 1], s.ag_r.at[k, d - 1], (node, j))
                copy.start()
                stage_copies.append(copy)
        agg_copies.append(stage_copies)

    for copy in wx_copies:
        copy.wait()
    other = (node_of(z, x, 1 - c), f)
    w_swap = remote(s.wq.at[c], s.wq.at[c], s.wsw.at[0], s.wsw.at[1], other)
    w_swap.start()
    w_swap.wait()
    for j in range(nf):
        for at in range(xs):
            for h in range(CORES):
                s.wfull[pl.ds(j * width + at * rows, rows), pl.ds(h * cols, cols)] = s.wq[h, at, j]
    s.wt[...] = s.wfull[...].T

    grad_copies = [[] for _ in range(plan.stages)]

    def send_grad(k, distances):
        for d in distances:
            j = lax.rem(f + d, nf)
            into = s.first.at[pl.ds(2 * f, 2)] if k == 0 else s.grad.at[pl.ds(2 * (k * nf + f), 2)]
            copy = remote(s.gsend.at[k, j], into, s.gr_s.at[k, d - 1], s.gr_r.at[k, d - 1], (node, j))
            copy.start()
            grad_copies[k].append(copy)

    for k in range(plan.stages):
        for copy in up_copies[k] + agg_copies[k]:
            copy.wait()
        if k:
            send_grad(k - 1, far_first)
        agg = s.ar[k].reshape(plan.full, pair)
        pre = jnp.dot(s.wt[...], agg, preferred_element_type=F32)
        sig = jax.nn.sigmoid(pre)
        upstream = s.ur[k].reshape(plan.full, pair).astype(F32)
        s.gp[...] = (upstream * sig * (1.0 + pre * (1.0 - sig))).astype(BF16)

        def weight_part(h):
            columns = s.gp[pl.ds(pl.multiple_of(h * cols, cols), cols)]
            wg = lax.dot_general(agg, columns, (((1,), (1,)), ((), ())), preferred_element_type=F32)
            return wg.reshape(nf, width, cols) + (s.wg[h] if k else 0.0)

        last = k == plan.stages - 1
        if last:
            s.wg0[...] = weight_part(1 - c).astype(BF16)
            wg_core = remote(s.wg0, s.wg_c, s.wc.at[0], s.wc.at[1], other)
            wg_core.start()
        grad = jnp.dot(s.wfull[...], s.gp[...], preferred_element_type=F32).astype(BF16)
        for j in range(nf):
            for h in range(2):
                s.gsend[k, j, h] = grad[j * width : (j + 1) * width, h * BLK : (h + 1) * BLK]
        if last:
            send_grad(k, far_first[HELD:])
        into = s.first.at[pl.ds(2 * f, 2)] if k == 0 else s.grad.at[pl.ds(2 * (k * nf + f), 2)]
        into[...] = s.gsend[k, f]
        if last:
            s.wg[c] = weight_part(c)
        else:
            for h in range(CORES):
                s.wg[h] = weight_part(h)

    wg_core.wait()
    x_copies = []
    for d in x_far_first + [0]:
        to_x = lax.rem(x + d, xs)
        at = pl.ds(pl.multiple_of(to_x * rows, rows), rows)
        part = s.wg[c, :, at, :] + s.wg_c[:, at, :].astype(F32)
        if d:
            s.wg1[d - 1] = part.astype(BF16)
            to = (node_of(z, to_x, c), f)
            copy = remote(s.wg1.at[d - 1], s.wg_x.at[d - 1], s.wx_s.at[d - 1], s.wx_r.at[d - 1], to)
            copy.start()
            x_copies.append(copy)
        else:
            s.wg2[...] = part
    for copy in x_copies:
        copy.wait_recv()
    s.wg2[...] = sum([s.wg_x[d].astype(F32) for d in range(xs - 1)], s.wg2[...])
    s.wg2b[...] = s.wg2[...].astype(BF16)
    y_copies = []
    for d in far_first:
        j = lax.rem(f + d, nf)
        copy = remote(s.wg2b.at[j], s.wg_y.at[d - 1], s.wy_s.at[d - 1], s.wy_r.at[d - 1], (node, j))
        copy.start()
        y_copies.append(copy)
    send_grad(plan.stages - 1, far_first[:HELD])
    for copy in grad_copies[0]:
        copy.wait()
    back_copies = []
    for i, d in enumerate(plan.offsets):
        term = jnp.dot(s.first[idx[BH_R, i]], s.tiles[idx[BH_T, i]], preferred_element_type=F32)
        s.bsend[i] = term.astype(BF16)
        copy = remote(
            s.bsend.at[i], s.brecv.at[i], s.back_s.at[i], s.back_r.at[i], (lax.rem(node + d + nn, nn), f)
        )
        copy.start()
        back_copies.append(copy)
    s.grad[pl.ds(0, 2 * nf)] = s.first[...]

    for copy in y_copies:
        copy.wait_recv()
    s.wg3[...] = sum([s.wg_y[d].astype(F32) for d in range(nf - 1)], s.wg2[f]).astype(BF16)
    s.wg_z[z] = s.wg3[...]
    z_copies = []
    for d in z_far_first:
        to = (node_of(lax.rem(z + d, zs), x, c), f)
        copy = remote(s.wg3, s.wg_z.at[z], s.wz_s.at[d - 1], s.wz_r.at[d - 1], to)
        copy.start()
        z_copies.append(copy)

    for copy in z_copies:
        copy.wait_recv()
    s.wg4[...] = sum([s.wg_z[at].astype(F32) for at in range(1, zs)], s.wg_z[0].astype(F32))
    s.wg5[c, x] = s.wg4[...]
    last_copies = []
    for i, (dx, dc) in enumerate(plane):
        to = (node_of(z, lax.rem(x + dx, xs), lax.rem(c + dc, CORES)), f)
        copy = remote(s.wg4, s.wg5.at[c, x], s.wl_s.at[i], s.wl_r.at[i], to)
        copy.start()
        last_copies.append(copy)

    for copy in sum(grad_copies[1:], []):
        copy.wait()

    def backward_local(i, total):
        keep = idx[BL_K, i].astype(F32)
        term = jnp.dot(s.grad[idx[BL_R, i]], s.tiles[idx[BL_T, i]], preferred_element_type=F32)
        total = total * keep + term
        s.bsum[i + 1] = total
        return total

    lax.fori_loop(0, plan.local, backward_local, zero, unroll=16)

    for copy in back_copies:
        copy.wait()

    def returned(i, total):
        keep = idx[R_K, i].astype(F32)
        total = total * keep + s.brecv[idx[R_S, i]].astype(F32)
        s.rsum[i + 1] = total
        return total

    lax.fori_loop(0, plan.halo, returned, zero, unroll=plan.halo)

    for b in range(plan.blocks):
        out_ref[:, b * BLK : (b + 1) * BLK] = (s.bsum[idx[BL_END, b]] + s.rsum[idx[R_END, b]]).astype(BF16)

    for copy in x_copies + y_copies + z_copies:
        copy.wait_send()
    for copy in last_copies:
        copy.wait()
    for h in range(CORES):
        for at in range(xs):
            wout_ref[pl.ds(at * rows, rows), pl.ds(h * cols, cols)] = s.wg5[h, at]


class Scratch:
    pass


def scratch_of(plan):
    nf, ns, halo, blocks, width = plan.feats, plan.stages, plan.halo, plan.blocks, plan.width
    cols, rows = plan.full // CORES, width // plan.xs
    dma = pltpu.SemaphoreType.DMA
    vmem = pltpu.VMEM
    return {
        "feats": vmem((width, blocks * BLK), BF16),
        "table": vmem((blocks + 1, width, BLK), BF16),
        "up": vmem((width, blocks * BLK), BF16),
        "uptable": vmem((blocks, width, BLK), BF16),
        "upk": vmem((blocks // 2, width, 2 * BLK), BF16),
        "ur": vmem((ns, nf, width, 2 * BLK), BF16),
        "wq": vmem((CORES, plan.xs, nf, rows, cols), BF16),
        "wfull": vmem((plan.full, plan.full), BF16),
        "wt": vmem((plan.full, plan.full), BF16),
        "tiles": vmem((plan.tiles, BLK, BLK), BF16),
        "hsend": vmem((halo, width, BLK), BF16),
        "hrecv": vmem((halo, width, BLK), BF16),
        "fsum": vmem((plan.local + 1, width, BLK), F32),
        "hsum": vmem((halo + 1, width, BLK), F32),
        "apk": vmem((blocks // 2, width, 2 * BLK), BF16),
        "ar": vmem((ns, nf, width, 2 * BLK), BF16),
        "gp": vmem((plan.full, 2 * BLK), BF16),
        "gsend": vmem((ns, nf, 2, width, BLK), BF16),
        "first": vmem((2 * nf, width, BLK), BF16),
        "grad": vmem((blocks + 1, width, BLK), BF16),
        "send_sm": pltpu.SMEM((1, plan.nodes), jnp.int32),
        "send_v": vmem((1, plan.nodes), jnp.int32),
        "row_v": vmem((1, plan.tiles), jnp.int32),
        "col_v": vmem((1, plan.tiles), jnp.int32),
        "count_v": vmem((1, 1), jnp.int32),
        "get_small": dma((5,)),
        "line": vmem((8, LANES), jnp.int32),
        "order_v": vmem((8, LANES), jnp.int32),
        "order": pltpu.SMEM((8, LANES), jnp.int32),
        "lists": vmem((LISTS, LANES), jnp.int32),
        "idx": pltpu.SMEM((LISTS, LANES), jnp.int32),
        "wg": vmem((CORES, nf, width, cols), F32),
        "wg0": vmem((nf, width, cols), BF16),
        "wg_c": vmem((nf, width, cols), BF16),
        "wg1": vmem((plan.xs - 1, nf, rows, cols), BF16),
        "wg_x": vmem((plan.xs - 1, nf, rows, cols), BF16),
        "wg2": vmem((nf, rows, cols), F32),
        "wg2b": vmem((nf, rows, cols), BF16),
        "wg_z": vmem((plan.zs, rows, cols), BF16),
        "wg3": vmem((rows, cols), BF16),
        "wg_y": vmem((nf - 1, rows, cols), BF16),
        "wg4": vmem((rows, cols), F32),
        "wg5": vmem((CORES, plan.xs, rows, cols), F32),
        "bsend": vmem((halo, width, BLK), BF16),
        "brecv": vmem((halo, width, BLK), BF16),
        "bsum": vmem((plan.local + 1, width, BLK), F32),
        "rsum": vmem((halo + 1, width, BLK), F32),
        "get": dma((6,)),
        "halo_s": dma((halo,)), "halo_r": dma((halo,)),
        "w_s": dma((nf - 1,)), "w_r": dma((nf - 1,)),
        "wqx_s": dma((plan.xs - 1,)), "wqx_r": dma((plan.xs - 1,)),
        "wsw": dma((2,)),
        "up_s": dma((ns, nf - 1)), "up_r": dma((ns, nf - 1)),
        "ag_s": dma((ns, nf - 1)), "ag_r": dma((ns, nf - 1)),
        "gr_s": dma((ns, nf - 1)), "gr_r": dma((ns, nf - 1)),
        "back_s": dma((halo,)), "back_r": dma((halo,)),
        "wc": dma((2,)),
        "wx_s": dma((plan.xs - 1,)), "wx_r": dma((plan.xs - 1,)),
        "wz_s": dma((plan.zs - 1,)), "wz_r": dma((plan.zs - 1,)),
        "wy_s": dma((nf - 1,)), "wy_r": dma((nf - 1,)),
        "wl_s": dma((CORES * plan.xs - 1,)), "wl_r": dma((CORES * plan.xs - 1,)),
    }


def local(offsets_of, x_chips, features, weight, tile_row, tile_col, tile_count, send_blocks, tile_values, upstream):
    rows_dev, width = features.shape
    blocks = rows_dev // BLK
    nodes, feats = lax.axis_size("node"), lax.axis_size("feat")
    plan = Plan(blocks, width, tile_row.shape[0], feats, nodes, offsets_of(nodes), x_chips)
    scratch = scratch_of(plan)
    names = list(scratch)
    given = 8

    def body(*refs):
        s = Scratch()
        for name, ref in zip(names, refs[given + 2 :]):
            setattr(s, name, ref)
        kernel(plan, *refs[: given + 2], s)

    anywhere = pl.BlockSpec(memory_space=pltpu.HBM)
    in_vmem = pl.BlockSpec(memory_space=pltpu.VMEM)
    grad_t, weight_sum = pl.pallas_call(
        body,
        out_shape=(
            pltpu.VMEM((width, rows_dev), BF16),
            pltpu.VMEM((width, plan.full), F32),
        ),
        in_specs=[anywhere] * given,
        out_specs=(in_vmem, in_vmem),
        scratch_shapes=[scratch[name] for name in names],
        compiler_params=pltpu.CompilerParams(
            collective_id=0, has_side_effects=True, vmem_limit_bytes=62 * 1024 * 1024
        ),
    )(
        tile_count.reshape(1, 1), send_blocks.reshape(1, nodes), tile_row.reshape(1, -1), tile_col.reshape(1, -1),
        features.T, upstream.T, weight, tile_values,
    )
    return grad_t.T, weight_sum / math.sqrt(rows_dev * nodes)


def build(mesh, offsets_of, x_chips):
    in_specs = (
        P("node", "feat"),
        P("feat", None),
        P("node"),
        P("node"),
        P("node"),
        P("node", None, None),
        P("node", None, None),
        P("node", "feat"),
    )
    out_specs = (P("node", "feat"), P("feat", None))
    return jax.shard_map(
        functools.partial(local, offsets_of, x_chips), mesh=mesh, in_specs=in_specs, out_specs=out_specs, check_vma=False
    )


def solution(mesh):
    return build(mesh, halo_offsets, X_CHIPS)
```
